256 devices in a mesh: dp: 16 (over z, core), tensor: 16 (over x, y).
Axes of the slice: x: 4, y: 4, z: 8, core: 2. Of those that a mesh axis runs over, the one named last changes fastest.
Arguments:
- gate_grad: bfloat16 [16, 2048, 4096], P('dp', 'tensor'), may hold values from -6 to 6
- gate_scale: float32 [16, 2048, 32], P('dp', 'tensor'), may hold values from 0.4 to 8
- gate_error: bfloat16 [16, 2048, 4096], P('dp', 'tensor'), may hold values from -6 to 6
- gate_prior: float32 [4096, 32], replicated, may hold values from -6 to 6
- up_grad: bfloat16 [16, 2048, 4096], P('dp', 'tensor'), may hold values from -6 to 6
- up_scale: float32 [16, 2048, 32], P('dp', 'tensor'), may hold values from 0.4 to 8
- up_error: bfloat16 [16, 2048, 4096], P('dp', 'tensor'), may hold values from -6 to 6
- up_prior: float32 [4096, 32], replicated, may hold values from -6 to 6
Outputs:
- gate_columns: float32 [4096, 32], replicated
- up_columns: float32 [4096, 32], replicated
- gate_update: bfloat16 [2048, 4096], P('tensor')
- up_update: bfloat16 [2048, 4096], P('tensor')
- gate_residue: bfloat16 [16, 2048, 4096], P('dp', 'tensor')
- up_residue: bfloat16 [16, 2048, 4096], P('dp', 'tensor')
The draws below stay inside these ranges and needn't reach their ends.
All inputs are finite; a program needn't handle non-finite values.
Results may differ from the reference program's by a relative error of at most 0.001.
Values sent between devices are 32-bit elements; how exact they have to be, the bound alone decides.
A program may use at most 64 MiB of HBM per device.

```python
import math
import jax
import jax.numpy as jnp
from jax import lax

D = 4096
RANK = 32
BLOCK = 128
ROWS = 2048
REPLICAS = 16


def steps_of(stream_key, shape, split, low, top_value):
    def one(position, blocks):
        steps = jax.random.uniform(jax.random.fold_in(jax.random.fold_in(stream_key, 6), position), (blocks,), jnp.float32, low / len(split), top_value / len(split))
        return jnp.repeat(jnp.exp(steps), shape[position] // blocks).reshape((-1,) + (1,) * (len(shape) - position - 1))

    factor_of = one(*split[0])
    for cut in split[1:]:
        factor_of = factor_of * one(*cut)
    return factor_of


def centred(rng, shape, spread, most, pieces=(), kind=jnp.bfloat16):
    result = jax.random.normal(rng, shape, jnp.float32) * spread
    if len(pieces) > 0:
        result = steps_of(rng, shape, pieces, -0.22, 0.18) * result
    return jnp.clip(result, min=-most, max=most).astype(kind)


def setup_inputs(seed: int = 0) -> dict:
    splits = jax.random.split(jax.random.key(seed), 9)
    gate_grad = centred(splits[0], (REPLICAS, ROWS, D), 1.0, 6.0, ((0, 16), (1, 16)))
    gate_scale = jnp.clip(jnp.exp(math.log(8.0) - 2.9957323 * jax.random.uniform(splits[1], (REPLICAS, ROWS, D // BLOCK), jnp.float32) ** steps_of(splits[1], (REPLICAS, ROWS, D // BLOCK), ((0, 16), (1, 16)), -0.2, 0.2)), 0.4, 8.0)
    gate_error = centred(splits[2], (REPLICAS, ROWS, D), 1.0, 6.0, ((0, 16), (1, 16)))
    gate_prior = centred(splits[3], (D, RANK), 1.0, 6.0, (), jnp.float32)
    up_grad = centred(splits[4], (REPLICAS, ROWS, D), 1.0, 6.0, ((0, 16), (1, 16)))
    up_scale = jnp.clip(jnp.exp(math.log(8.0) - 2.9957323 * jax.random.uniform(splits[5], (REPLICAS, ROWS, D // BLOCK), jnp.float32) ** steps_of(splits[5], (REPLICAS, ROWS, D // BLOCK), ((0, 16), (1, 16)), -0.2, 0.2)), 0.4, 8.0)
    up_error = centred(splits[6], (REPLICAS, ROWS, D), 1.0, 6.0, ((0, 16), (1, 16)))
    up_prior = centred(splits[7], (D, RANK), 1.0, 6.0, (), jnp.float32)
    return dict(gate_grad=gate_grad, gate_scale=gate_scale, gate_error=gate_error, gate_prior=gate_prior, up_grad=up_grad, up_scale=up_scale, up_error=up_error, up_prior=up_prior)


def expand(grad, scale):
    blocks = scale.shape[-1]
    width = grad.shape[-1] // blocks
    values = grad.astype(jnp.float32).reshape(grad.shape[:-1] + (blocks, width))
    return (values * scale[..., None]).reshape(grad.shape)

def settle(grad, scale, error, prior):
    count = grad.shape[0]
    indices = jnp.arange(count, dtype=jnp.int32)

    def work_of(replica):
        return expand(grad[replica], scale[replica]) + error[replica].astype(jnp.float32)

    def add_factor(total, replica):
        return (total + jnp.dot(work_of(replica), prior, precision=lax.Precision.HIGHEST), None)
    factor, unused = lax.scan(add_factor, jnp.zeros((grad.shape[1], prior.shape[1]), jnp.float32), indices)
    gram = jnp.dot(factor.T, factor, precision=lax.Precision.HIGHEST)
    lower_factor = jnp.linalg.cholesky(gram)
    basis = lax.linalg.triangular_solve(lower_factor, factor, left_side=False, lower=True, transpose_a=True)

    def add_column(total, replica):
        return (total + jnp.dot(work_of(replica).T, basis, precision=lax.Precision.HIGHEST), None)
    totals, unused = lax.scan(add_column, jnp.zeros((grad.shape[2], prior.shape[1]), jnp.float32), indices)
    columns = totals / count
    approx = jnp.dot(basis, columns.T, precision=lax.Precision.HIGHEST)

    def residue_of(replica):
        return (work_of(replica) - approx).astype(jnp.bfloat16)
    residue = lax.map(residue_of, indices)
    return (columns, approx.astype(jnp.bfloat16), residue)

def reference(gate_grad, gate_scale, gate_error, gate_prior, up_grad, up_scale, up_error, up_prior):
    gate_columns, gate_update, gate_residue = settle(gate_grad, gate_scale, gate_error, gate_prior)
    up_columns, up_update, up_residue = settle(up_grad, up_scale, up_error, up_prior)
    return (gate_columns, up_columns, gate_update, up_update, gate_residue, up_residue)
```

```python
import functools

import jax
import jax.numpy as jnp
from jax import lax
from jax.experimental import pallas as pl
from jax.experimental.pallas import tpu as pltpu
from jax.sharding import PartitionSpec as P

MESH = pl.DeviceIdType.MESH
F32 = jnp.float32
BF16 = jnp.bfloat16

ROWS = 128
COLS = 4096
RANK = 32
BLOCK = 128
NZ = 8
NXY = 16
HALVES = 2
SPAN = COLS // HALVES
PIECE = SPAN // NXY
CHUNKS = 4
WIDTH = COLS // CHUNKS

NN = (((1,), (0,)), ((), ()))
NT = (((1,), (1,)), ((), ()))


def split2(a):
    hi = a.astype(BF16)
    lo = (a - hi.astype(F32)).astype(BF16)
    return hi, lo


def split3(a):
    hi = a.astype(BF16)
    rest = a - hi.astype(F32)
    mid = rest.astype(BF16)
    lo = (rest - mid.astype(F32)).astype(BF16)
    return hi, mid, lo


def mm(a, b, dims=NN):
    return lax.dot_general(a, b, dims, preferred_element_type=F32)


def exact(a, b, dims=NN):
    return lax.dot_general(a, b, dims, preferred_element_type=F32, precision=lax.Precision.HIGHEST)


def inverse_factor(gram):
    rows = lax.broadcasted_iota(jnp.int32, (RANK, 1), 0)
    eye = (lax.broadcasted_iota(jnp.int32, (RANK, RANK), 0) == lax.broadcasted_iota(jnp.int32, (RANK, RANK), 1)).astype(F32)
    left, right = gram, eye
    roots = jnp.zeros((RANK, 1), F32)
    for j in range(RANK):
        pivot = left[j : j + 1, j : j + 1]
        roots = jnp.where(rows == j, lax.rsqrt(pivot), roots)
        factor = jnp.where(rows > j, left[:, j : j + 1] / pivot, 0.0)
        left = left - factor * left[j : j + 1, :]
        right = right - factor * right[j : j + 1, :]
    return right * roots


def total_wait(ref, sem):
    pltpu.make_async_copy(ref, ref, sem).wait()


def exchange_kernel(
    g0, s0, e0, p0, g1, s1, e1, p1,
    columns0, columns1, basis,
    g_buf, e_buf, s_buf, p_buf, w_hi, w_lo,
    f_part, f_pair, f_own, f_z, f_all, gram_own, gram_xy,
    t_own, t_pair, t_xy, t_z, piece,
    in_sems, pair_send, pair_recv, z_send, z_recv, xy_send, xy_recv, t_send, t_recv,
):
    dp = lax.axis_index("dp")
    me = lax.axis_index("tensor")
    z, c = dp // 2, dp % 2
    x, y = me // 4, me % 4
    other = 1 - c
    sibling = {"dp": z * 2 + other, "tensor": me}
    z_peers = [{"dp": lax.rem(z + k, NZ) * 2 + c, "tensor": me} for k in (4, 3, 5, 2, 6, 1, 7)]
    xy_index = [
        lax.rem(x + dx, 4) * 4 + lax.rem(y + dy, 4)
        for dx, dy in sorted(
            ((i, j) for i in range(4) for j in range(4) if i or j),
            key=lambda d: -(min(d[0], 4 - d[0]) + min(d[1], 4 - d[1])),
        )
    ]
    xy_peers = [{"dp": dp, "tensor": t} for t in xy_index]

    barrier = pltpu.get_barrier_semaphore()
    for peer in [sibling] + z_peers + xy_peers:
        pl.semaphore_signal(barrier, inc=1, device_id=peer, device_id_type=MESH)

    small = []
    for m, (s, p) in enumerate(((s0, p0), (s1, p1))):
        small.append(pltpu.make_async_copy(s.at[0], s_buf.at[m], in_sems.at[m, 0]))
        small.append(pltpu.make_async_copy(p, p_buf.at[m], in_sems.at[m, 1]))
    for copy in small:
        copy.start()
    big = {}
    for m, (g, e) in enumerate(((g0, e0), (g1, e1))):
        for k in range(CHUNKS):
            cols = pl.ds(k * WIDTH, WIDTH)
            big[m, k] = (
                pltpu.make_async_copy(g.at[0, :, cols], g_buf.at[m, :, cols], in_sems.at[m, 2 + 2 * k]),
                pltpu.make_async_copy(e.at[0, :, cols], e_buf.at[m, :, cols], in_sems.at[m, 3 + 2 * k]),
            )
            for copy in big[m, k]:
                copy.start()
    for copy in small:
        copy.wait()

    for m in range(2):
        scale = s_buf[m].T
        total = jnp.zeros((ROWS, 3 * RANK), F32)
        for k in range(CHUNKS):
            for copy in big[m, k]:
                copy.wait()
            for b in range(k * WIDTH // BLOCK, (k + 1) * WIDTH // BLOCK):
                cols = slice(b * BLOCK, (b + 1) * BLOCK)
                work = g_buf[m, :, cols].astype(F32) * scale[:, b : b + 1] + e_buf[m, :, cols].astype(F32)
                hi, lo = split2(work)
                w_hi[m, :, cols] = hi
                w_lo[m, :, cols] = lo
            cols = slice(k * WIDTH, (k + 1) * WIDTH)
            prior = jnp.concatenate(split3(p_buf[m, :, cols]), 0)
            total = total + mm(w_hi[m, :, cols], prior, NT) + mm(w_lo[m, :, cols], prior, NT)
        factor = total[:, :RANK] + (total[:, RANK : 2 * RANK] + total[:, 2 * RANK :])
        f_part[m] = factor.T

    pl.semaphore_wait(barrier, 1 + len(z_peers) + len(xy_peers))

    sends = []

    def send(src, dst, send_sem, recv_sem, peer):
        copy = pltpu.make_async_remote_copy(
            src_ref=src, dst_ref=dst, send_sem=send_sem, recv_sem=recv_sem, device_id=peer, device_id_type=MESH
        )
        copy.start()
        return copy

    first = send(f_part.at[other], f_pair, pair_send.at[0], pair_recv.at[0], sibling)
    sends.append(first)
    first.wait_recv()
    f_own[...] = f_part[c] + f_pair[...]
    f_z[z] = f_own[...]

    for peer in z_peers:
        send(f_own, f_z.at[z], z_send.at[0], z_recv.at[0], peer)
    total_wait(f_z.at[pl.ds(0, NZ - 1)], z_recv.at[0])
    mine = f_z[0]
    for k in range(1, NZ):
        mine = mine + f_z[k]
    f_all[c] = mine
    second = send(f_all.at[c], f_all.at[c], pair_send.at[1], pair_recv.at[1], sibling)
    sends.append(second)

    gram = exact(mine, mine, NT)
    gram_own[...] = jnp.concatenate([gram, jnp.zeros((RANK, 128 - RANK), F32)], 1)
    gram_xy[me] = gram_own[...]
    for peer in xy_peers:
        send(gram_own, gram_xy.at[me], xy_send.at[0], xy_recv.at[0], peer)

    def terms(m, factor, span):
        hi, lo = split2(factor)
        zero = jnp.zeros_like(lo)
        lhs = jnp.concatenate([jnp.concatenate([hi, hi], 1), jnp.concatenate([lo, zero], 1)], 0)
        rhs = jnp.concatenate([w_hi[m, :, span], w_lo[m, :, span]], 0)
        both = mm(lhs, rhs)
        return both[:RANK] + both[RANK:]

    for h in range(HALVES):
        t_own[h] = terms(c, mine, pl.ds(h * SPAN, SPAN))
    second.wait_recv()
    theirs = f_all[other]
    pair_copies = []
    for h in range(HALVES):
        t_pair[0, h] = terms(other, theirs, pl.ds(h * SPAN, SPAN))
        pair_copies.append(send(t_pair.at[0, h], t_pair.at[1, h], pair_send.at[2 + h], pair_recv.at[2 + h], sibling))
    sends += pair_copies

    for h in range(HALVES):
        pair_copies[h].wait_recv()
        t_own[h] = t_own[h] + t_pair[1, h]
        for t, peer in zip(xy_index, xy_peers):
            cols = pl.ds(pl.multiple_of(t * PIECE, PIECE), PIECE)
            send(t_own.at[h, :, cols], t_xy.at[h, me], t_send.at[0, h], t_recv.at[0, h], peer)
        t_xy[h, me] = t_own[h, :, pl.ds(pl.multiple_of(me * PIECE, PIECE), PIECE)]

    total_wait(gram_xy.at[pl.ds(0, NXY - 1)], xy_recv.at[0])
    gram = gram_xy[0]
    for k in range(1, NXY):
        gram = gram + gram_xy[k]
    inverse = inverse_factor(gram[:, :RANK])
    basis[c] = exact(inverse, mine)
    sends.append(send(basis.at[c], basis.at[c], pair_send.at[4], pair_recv.at[4], sibling))

    for h in range(HALVES):
        total_wait(t_xy.at[h, pl.ds(0, NXY - 1)], t_recv.at[0, h])
        part = t_xy[h, 0]
        for k in range(1, NXY):
            part = part + t_xy[h, k]
        piece[0, h] = part
        t_z[h, z] = part
        for peer in z_peers:
            send(piece.at[0, h], t_z.at[h, z], t_send.at[1, h], t_recv.at[1, h], peer)

    for h in range(HALVES):
        total_wait(t_z.at[h, pl.ds(0, NZ - 1)], t_recv.at[1, h])
        part = t_z[h, 0]
        for k in range(1, NZ):
            part = part + t_z[h, k]
        piece[1, h] = exact(inverse, part) * (1.0 / 16.0)
        cols = pl.ds(pl.multiple_of(h * SPAN + me * PIECE, PIECE), PIECE)

        @pl.when(c == 0)
        def _():
            columns0[:, cols] = piece[1, h]
            for peer in xy_peers:
                send(piece.at[1, h], columns0.at[:, cols], t_send.at[2, h], t_recv.at[2, h], peer)

        @pl.when(c == 1)
        def _():
            columns1[:, cols] = piece[1, h]
            for peer in xy_peers:
                send(piece.at[1, h], columns1.at[:, cols], t_send.at[2, h], t_recv.at[2, h], peer)

    for h in range(HALVES):
        total_wait(t_xy.at[h, pl.ds(0, NXY - 1)], t_recv.at[2, h])
        cols = pl.ds(h * SPAN, SPAN)

        @pl.when(c == 0)
        def _():
            send(columns0.at[:, cols], columns0.at[:, cols], pair_send.at[5 + h], pair_recv.at[5 + h], sibling)

        @pl.when(c == 1)
        def _():
            send(columns1.at[:, cols], columns1.at[:, cols], pair_send.at[5 + h], pair_recv.at[5 + h], sibling)

    for h in range(HALVES):
        total_wait(t_own.at[h], pair_recv.at[5 + h])
        total_wait(t_own.at[h], pair_send.at[5 + h])
    sends[-1].wait_recv()
    for copy in sends:
        copy.wait_send()
    total_wait(f_z.at[pl.ds(0, NZ - 1)], z_send.at[0])
    total_wait(gram_xy.at[pl.ds(0, NXY - 1)], xy_send.at[0])
    for h in range(HALVES):
        total_wait(t_xy.at[h, pl.ds(0, NXY - 1)], t_send.at[0, h])
        total_wait(t_z.at[h, pl.ds(0, NZ - 1)], t_send.at[1, h])
        total_wait(t_xy.at[h, pl.ds(0, NXY - 1)], t_send.at[2, h])


def exchange(*args):
    vmem, sems = pltpu.VMEM, pltpu.SemaphoreType.DMA
    return pl.pallas_call(
        exchange_kernel,
        out_shape=(
            jax.ShapeDtypeStruct((RANK, COLS), F32),
            jax.ShapeDtypeStruct((RANK, COLS), F32),
            jax.ShapeDtypeStruct((2, RANK, ROWS), F32),
        ),
        in_specs=[pl.BlockSpec(memory_space=pl.ANY)] * 8,
        out_specs=[pl.BlockSpec(memory_space=pltpu.VMEM)] * 3,
        scratch_shapes=[
            vmem((2, ROWS, COLS), BF16),
            vmem((2, ROWS, COLS), BF16),
            vmem((2, COLS // BLOCK, ROWS), F32),
            vmem((2, RANK, COLS), F32),
            vmem((2, ROWS, COLS), BF16),
            vmem((2, ROWS, COLS), BF16),
            vmem((2, RANK, ROWS), F32),
            vmem((RANK, ROWS), F32),
            vmem((RANK, ROWS), F32),
            vmem((NZ, RANK, ROWS), F32),
            vmem((2, RANK, ROWS), F32),
            vmem((RANK, 128), F32),
            vmem((NXY, RANK, 128), F32),
            vmem((HALVES, RANK, SPAN), F32),
            vmem((2, HALVES, RANK, SPAN), F32),
            vmem((HALVES, NXY, RANK, PIECE), F32),
            vmem((HALVES, NZ, RANK, PIECE), F32),
            vmem((2, HALVES, RANK, PIECE), F32),
            sems((2, 2 + 2 * CHUNKS)),
            sems((5 + HALVES,)),
            sems((5 + HALVES,)),
            sems((1,)),
            sems((1,)),
            sems((1,)),
            sems((1,)),
            sems((3, HALVES)),
            sems((3, HALVES)),
        ],
        compiler_params=pltpu.CompilerParams(collective_id=0, has_side_effects=True, vmem_limit_bytes=28 << 20),
        cost_estimate=pl.CostEstimate(flops=1 << 30, bytes_accessed=8 << 20, transcendentals=0),
    )(*args)


def finish_kernel(
    g0, s0, e0, g1, s1, e1, columns0, columns1, basis,
    out0, out1, update0, update1, residue0, residue1,
):
    step = pl.program_id(0)
    for m, (g, s, e, columns, out, update, residue) in enumerate(
        ((g0, s0, e0, columns0, out0, update0, residue0), (g1, s1, e1, columns1, out1, update1, residue1))
    ):
        block = columns[...]
        out[...] = block
        approx = exact(basis[m].T, block)
        update[...] = approx.astype(BF16)
        width = block.shape[1]
        count = width // BLOCK
        scale = s[0, pl.ds(pl.multiple_of(step * count, count), count), :].T
        for b in range(count):
            cols = slice(b * BLOCK, (b + 1) * BLOCK)
            work = g[0, :, cols].astype(F32) * scale[:, b : b + 1] + e[0, :, cols].astype(F32)
            residue[0, :, cols] = (work - approx[:, cols]).astype(BF16)


def finish(g0, s0, e0, g1, s1, e1, columns0, columns1, basis):
    width = 1024
    grad = pl.BlockSpec((1, ROWS, width), lambda i: (0, 0, i))
    scale = pl.BlockSpec((1, COLS // BLOCK, ROWS), lambda i: (0, 0, 0))
    column = pl.BlockSpec((RANK, width), lambda i: (0, i))
    wide = pl.BlockSpec((ROWS, width), lambda i: (0, i))
    return pl.pallas_call(
        finish_kernel,
        grid=(COLS // width,),
        out_shape=(
            jax.ShapeDtypeStruct((RANK, COLS), F32),
            jax.ShapeDtypeStruct((RANK, COLS), F32),
            jax.ShapeDtypeStruct((ROWS, COLS), BF16),
            jax.ShapeDtypeStruct((ROWS, COLS), BF16),
            jax.ShapeDtypeStruct((1, ROWS, COLS), BF16),
            jax.ShapeDtypeStruct((1, ROWS, COLS), BF16),
        ),
        in_specs=[grad, scale, grad, grad, scale, grad, column, column, pl.BlockSpec((2, RANK, ROWS), lambda i: (0, 0, 0))],
        out_specs=[column, column, wide, wide, grad, grad],
        compiler_params=pltpu.CompilerParams(vmem_limit_bytes=28 << 20),
    )(g0, s0, e0, g1, s1, e1, columns0, columns1, basis)


def shards(gate_grad, gate_scale, gate_error, gate_prior, up_grad, up_scale, up_error, up_prior):
    s0, s1 = (s.transpose(0, 2, 1) for s in (gate_scale, up_scale))
    columns0, columns1, basis = exchange(
        gate_grad, s0, gate_error, gate_prior.T, up_grad, s1, up_error, up_prior.T
    )
    columns0, columns1, update0, update1, residue0, residue1 = finish(
        gate_grad, s0, gate_error, up_grad, s1, up_error, columns0, columns1, basis
    )
    return (columns0.T, columns1.T, update0, update1, residue0, residue1)


def solution(mesh):
    in_specs = (
        P("dp", "tensor", None),
        P("dp", "tensor", None),
        P("dp", "tensor", None),
        P(),
        P("dp", "tensor", None),
        P("dp", "tensor", None),
        P("dp", "tensor", None),
        P(),
    )
    out_specs = (
        P(),
        P(),
        P("tensor", None),
        P("tensor", None),
        P("dp", "tensor", None),
        P("dp", "tensor", None),
    )
    return jax.shard_map(shards, mesh=mesh, in_specs=in_specs, out_specs=out_specs, check_vma=False)
```

```python
import jax
import jax.numpy as jnp
from jax import lax
from jax.experimental import pallas as pl
from jax.experimental.pallas import tpu as pltpu
from jax.sharding import PartitionSpec as P

MESH = pl.DeviceIdType.MESH
F32 = jnp.float32
BF16 = jnp.bfloat16

ROWS = 128
COLS = 4096
RANK = 32
BLOCK = 128
NZ = 8
NXY = 16
PARTS = 4
RANKS = RANK // PARTS
PIECE = COLS // NXY
CHUNKS = 4
WIDTH = COLS // CHUNKS
SLICES = 8
SLICE = COLS // SLICES

NN = (((1,), (0,)), ((), ()))
NT = (((1,), (1,)), ((), ()))


def split2(a):
    hi = a.astype(BF16)
    lo = (a - hi.astype(F32)).astype(BF16)
    return hi, lo


def split3(a):
    hi = a.astype(BF16)
    rest = a - hi.astype(F32)
    mid = rest.astype(BF16)
    lo = (rest - mid.astype(F32)).astype(BF16)
    return hi, mid, lo


def mm(a, b, dims=NN):
    return lax.dot_general(a, b, dims, preferred_element_type=F32)


def exact(a, b, dims=NN):
    return lax.dot_general(a, b, dims, preferred_element_type=F32, precision=lax.Precision.HIGHEST)


def inverse_factor(gram):
    rows = lax.broadcasted_iota(jnp.int32, (RANK, 1), 0)
    eye = (lax.broadcasted_iota(jnp.int32, (RANK, RANK), 0) == lax.broadcasted_iota(jnp.int32, (RANK, RANK), 1)).astype(F32)
    left, right = gram, eye
    roots = jnp.zeros((RANK, 1), F32)
    for j in range(RANK):
        pivot = left[j : j + 1, j : j + 1]
        roots = jnp.where(rows == j, lax.rsqrt(pivot), roots)
        factor = jnp.where(rows > j, left[:, j : j + 1] / pivot, 0.0)
        left = left - factor * left[j : j + 1, :]
        right = right - factor * right[j : j + 1, :]
    return right * roots


def total_wait(ref, sem):
    pltpu.make_async_copy(ref, ref, sem).wait()


def send(ref, dst, send_sem, recv_sem, peer):
    pltpu.make_async_remote_copy(
        src_ref=ref, dst_ref=dst, send_sem=send_sem, recv_sem=recv_sem, device_id=peer, device_id_type=MESH
    ).start()


def loop(count, body):
    lax.fori_loop(0, count, lambda i, carry: (body(i), carry)[1], 0)


def exchange_kernel(
    g0, s0, e0, p0, g1, s1, e1, p1,
    columns, left, work,
    g_buf, e_buf, s_buf, p_buf, w_hi, w_lo,
    f_part, f_pair, f_z, f_all, gram_xy, inverse_ref, basis, summed,
    t_own, t_out, t_pair, t_xy, t_z,
    small_sems, in_sems, one_send, one_recv, fz_send, fz_recv, fp_send, fp_recv, tp_send, tp_recv,
    rs_send, rs_recv, tz_send, tz_recv, ag_send, ag_recv, cp_send, cp_recv,
):
    dp = lax.axis_index("dp")
    me = lax.axis_index("tensor")
    z, c = dp // 2, dp % 2
    x, y = me // 4, me % 4
    other = 1 - c
    sibling = {"dp": z * 2 + other, "tensor": me}

    def z_peer(i):
        return {"dp": lax.rem(z + 1 + lax.rem(i + 3, NZ - 1), NZ) * 2 + c, "tensor": me}

    def xy_index(i):
        k = 1 + lax.rem(i + 9, NXY - 1)
        return lax.rem(x + k // 4, 4) * 4 + lax.rem(y + k % 4, 4)

    def xy_peer(i):
        return {"dp": dp, "tensor": xy_index(i)}

    barrier = pltpu.get_barrier_semaphore()

    def greet(peer):
        pl.semaphore_signal(barrier, inc=1, device_id=peer, device_id_type=MESH)

    loop(NXY - 1, lambda i: greet(xy_peer(i)))
    loop(NZ - 1, lambda i: greet(z_peer(i)))
    greet(sibling)

    for m, (g, s, e, p) in enumerate(((g0, s0, e0, p0), (g1, s1, e1, p1))):
        pltpu.make_async_copy(s.at[0], s_buf.at[m], small_sems.at[m, 0]).start()
        pltpu.make_async_copy(p, p_buf.at[m], small_sems.at[m, 1]).start()

        def fetch(k):
            cols = pl.ds(pl.multiple_of(k * WIDTH, WIDTH), WIDTH)
            pltpu.make_async_copy(g.at[0, :, cols], g_buf.at[m, :, cols], in_sems.at[m, k, 0]).start()
            pltpu.make_async_copy(e.at[0, :, cols], e_buf.at[m, :, cols], in_sems.at[m, k, 1]).start()

        loop(CHUNKS, fetch)

    def partial(m):
        total_wait(s_buf.at[m], small_sems.at[m, 0])
        total_wait(p_buf.at[m], small_sems.at[m, 1])

        def chunk(k, total):
            cols = pl.ds(pl.multiple_of(k * WIDTH, WIDTH), WIDTH)
            total_wait(g_buf.at[m, :, cols], in_sems.at[m, k, 0])
            total_wait(e_buf.at[m, :, cols], in_sems.at[m, k, 1])
            count = WIDTH // BLOCK
            scale = s_buf[m, pl.ds(pl.multiple_of(k * count, count), count), :].T
            for b in range(count):
                at = pl.ds(pl.multiple_of(k * WIDTH + b * BLOCK, BLOCK), BLOCK)
                value = g_buf[m, :, at].astype(F32) * scale[:, b : b + 1] + e_buf[m, :, at].astype(F32)
                work[m, :, at] = value
                hi, lo = split2(value)
                w_hi[m, :, at] = hi
                w_lo[m, :, at] = lo
            prior = jnp.concatenate(split3(p_buf[m, :, cols]), 0)
            return total + mm(w_hi[m, :, cols], prior, NT) + mm(w_lo[m, :, cols], prior, NT)

        total = lax.fori_loop(0, CHUNKS, chunk, jnp.zeros((ROWS, 3 * RANK), F32))
        factor = total[:, :RANK] + (total[:, RANK : 2 * RANK] + total[:, 2 * RANK :])
        f_part[m] = factor.T

    loop(2, partial)
    summed[...] = jnp.zeros_like(summed)

    pl.semaphore_wait(barrier, 1 + (NZ - 1) + (NXY - 1))

    send(f_part.at[other], f_pair, one_send.at[0], one_recv.at[0], sibling)
    total_wait(f_pair, one_recv.at[0])
    for q in range(PARTS):
        rows = slice(q * RANKS, (q + 1) * RANKS)
        f_z[q, z] = f_part[c, rows] + f_pair[rows]

    def spread(q):
        loop(NZ - 1, lambda i: send(f_z.at[q, z], f_z.at[q, z], fz_send.at[q], fz_recv.at[q], z_peer(i)))

    loop(PARTS, spread)

    def terms(m, q):
        hi, lo = split2(f_all[m, q])
        lhs = jnp.concatenate([jnp.concatenate([hi, hi], 1), jnp.concatenate([lo, jnp.zeros_like(lo)], 1)], 0)
        both = mm(lhs, jnp.concatenate([w_hi[m], w_lo[m]], 0))
        return both[:RANKS] + both[RANKS:]

    def flow(i):
        @pl.when(i < PARTS)
        def _():
            q = i
            total_wait(f_z.at[q, pl.ds(0, NZ - 1)], fz_recv.at[q])
            total = f_z[q, 0]
            for k in range(1, NZ):
                total = total + f_z[q, k]
            f_all[c, q] = total
            send(f_all.at[c, q], f_all.at[c, q], fp_send.at[q], fp_recv.at[q], sibling)
            t_own[q] = terms(c, q)

        @pl.when((i >= 1) & (i < PARTS + 1))
        def _():
            q = i - 1
            total_wait(f_all.at[other, q], fp_recv.at[q])
            t_out[q] = terms(other, q)
            send(t_out.at[q], t_pair.at[q], tp_send.at[q], tp_recv.at[q], sibling)

        @pl.when(i >= 2)
        def _():
            q = i - 2
            total_wait(t_pair.at[q], tp_recv.at[q])
            t_own[q] = t_own[q] + t_pair[q]

            def scatter(j):
                cols = pl.ds(pl.multiple_of(xy_index(j) * PIECE, PIECE), PIECE)
                send(t_own.at[q, :, cols], t_xy.at[q, me], rs_send.at[q], rs_recv.at[q], xy_peer(j))

            loop(NXY - 1, scatter)
            t_xy[q, me] = t_own[q, :, pl.ds(pl.multiple_of(me * PIECE, PIECE), PIECE)]

    loop(PARTS + 2, flow)

    mine = jnp.concatenate([f_all[c, q] for q in range(PARTS)], 0)
    gram = exact(mine, mine, NT)
    gram_xy[me] = jnp.concatenate([gram[q * RANKS : (q + 1) * RANKS] for q in range(PARTS)], 1)
    loop(NXY - 1, lambda j: send(gram_xy.at[me], gram_xy.at[me], one_send.at[1], one_recv.at[1], xy_peer(j)))

    def middle(q):
        total_wait(t_xy.at[q, pl.ds(0, NXY - 1)], rs_recv.at[q])
        total = t_xy[q, 0]
        for k in range(1, NXY):
            total = total + t_xy[q, k]
        t_z[q, z] = total
        loop(NZ - 1, lambda i: send(t_z.at[q, z], t_z.at[q, z], tz_send.at[q], tz_recv.at[q], z_peer(i)))

    loop(PARTS, middle)

    total_wait(gram_xy.at[pl.ds(0, NXY - 1)], one_recv.at[1])
    packed = gram_xy[0]
    for k in range(1, NXY):
        packed = packed + gram_xy[k]
    gram = jnp.concatenate([packed[:, q * RANK : (q + 1) * RANK] for q in range(PARTS)], 0)
    inverse = inverse_factor(gram)
    basis[c] = exact(inverse, mine)
    send(basis.at[c], basis.at[c], one_send.at[2], one_recv.at[2], sibling)
    hi, mid, lo = split3(inverse)
    stacked = jnp.concatenate([hi, hi, mid, hi, mid, lo], 1)
    for q in range(PARTS):
        inverse_ref[q] = stacked[q * RANKS : (q + 1) * RANKS].astype(F32)

    own_cols = pl.ds(pl.multiple_of(me * PIECE, PIECE), PIECE)

    def gather(q):
        total_wait(t_z.at[q, pl.ds(0, NZ - 1)], tz_recv.at[q])
        total = t_z[q, 0]
        for k in range(1, NZ):
            total = total + t_z[q, k]
        rows = pl.ds(pl.multiple_of(q * RANKS, RANKS), RANKS)
        summed[rows, :] = total
        hi, mid, lo = split3(summed[...])
        rhs = jnp.concatenate([hi, mid, hi, lo, mid, hi], 0)
        columns[c, rows, own_cols] = mm(inverse_ref[q].astype(BF16), rhs) * (1.0 / 16.0)
        piece = columns.at[c, rows, own_cols]
        loop(NXY - 1, lambda j: send(piece, piece, ag_send.at[q], ag_recv.at[q], xy_peer(j)))

    loop(PARTS, gather)

    total_wait(basis.at[other], one_recv.at[2])
    for m in range(2):
        hi, lo = split2(basis[m].T)
        left[m] = jnp.concatenate([hi, hi, lo], 1)

    def hand(q):
        total_wait(t_xy.at[q, pl.ds(0, NXY - 1)], ag_recv.at[q])
        rows = pl.ds(pl.multiple_of(q * RANKS, RANKS), RANKS)
        send(columns.at[c, rows], columns.at[c, rows], cp_send.at[q], cp_recv.at[q], sibling)

    loop(PARTS, hand)

    def drain(q):
        rows = pl.ds(pl.multiple_of(q * RANKS, RANKS), RANKS)
        total_wait(columns.at[c, rows], cp_recv.at[q])
        total_wait(columns.at[c, rows], cp_send.at[q])
        total_wait(f_z.at[q, pl.ds(0, NZ - 1)], fz_send.at[q])
        total_wait(f_all.at[c, q], fp_send.at[q])
        total_wait(t_out.at[q], tp_send.at[q])
        total_wait(t_xy.at[q, pl.ds(0, NXY - 1)], rs_send.at[q])
        total_wait(t_z.at[q, pl.ds(0, NZ - 1)], tz_send.at[q])
        total_wait(t_xy.at[q, pl.ds(0, NXY - 1)], ag_send.at[q])

    loop(PARTS, drain)
    total_wait(f_pair, one_send.at[0])
    total_wait(gram_xy.at[pl.ds(0, NXY - 1)], one_send.at[1])
    total_wait(basis.at[c], one_send.at[2])


def exchange(*args):
    vmem, sems = pltpu.VMEM, pltpu.SemaphoreType.DMA
    return pl.pallas_call(
        exchange_kernel,
        out_shape=(
            jax.ShapeDtypeStruct((2, RANK, COLS), F32),
            jax.ShapeDtypeStruct((2, ROWS, 3 * RANK), BF16),
            jax.ShapeDtypeStruct((2, ROWS, COLS), F32),
        ),
        in_specs=[pl.BlockSpec(memory_space=pltpu.HBM)] * 8,
        out_specs=[pl.BlockSpec(memory_space=pltpu.VMEM)] * 3,
        scratch_shapes=[
            vmem((2, ROWS, COLS), BF16),
            vmem((2, ROWS, COLS), BF16),
            vmem((2, COLS // BLOCK, ROWS), F32),
            vmem((2, RANK, COLS), F32),
            vmem((2, ROWS, COLS), BF16),
            vmem((2, ROWS, COLS), BF16),
            vmem((2, RANK, ROWS), F32),
            vmem((RANK, ROWS), F32),
            vmem((PARTS, NZ, RANKS, ROWS), F32),
            vmem((2, PARTS, RANKS, ROWS), F32),
            vmem((NXY, RANKS, RANK * PARTS), F32),
            vmem((PARTS, RANKS, 6 * RANK), F32),
            vmem((2, RANK, ROWS), F32),
            vmem((RANK, PIECE), F32),
            vmem((PARTS, RANKS, COLS), F32),
            vmem((PARTS, RANKS, COLS), F32),
            vmem((PARTS, RANKS, COLS), F32),
            vmem((PARTS, NXY, RANKS, PIECE), F32),
            vmem((PARTS, NZ, RANKS, PIECE), F32),
            sems((2, 2)),
            sems((2, CHUNKS, 2)),
            sems((3,)),
            sems((3,)),
        ]
        + [sems((PARTS,))] * 14,
        compiler_params=pltpu.CompilerParams(collective_id=0, has_side_effects=True, vmem_limit_bytes=28 << 20),
        cost_estimate=pl.CostEstimate(flops=1 << 30, bytes_accessed=8 << 20, transcendentals=0),
    )(*args)


def finish_kernel(
    columns, left, work,
    out0, out1, update0, update1, residue0, residue1,
    update_buf, residue_buf, column_sems, out_sems,
):
    outs = (out0, out1)
    for m in range(2):
        pltpu.make_async_copy(columns.at[m], outs[m], column_sems.at[m]).start()
    for m, (update, residue) in enumerate(((update0, residue0), (update1, residue1))):

        def part(k):
            cols = pl.ds(pl.multiple_of(k * SLICE, SLICE), SLICE)
            hi, lo = split2(columns[m, :, cols])
            approx = mm(left[m], jnp.concatenate([hi, lo, hi], 0))
            update_buf[m, :, cols] = approx.astype(BF16)
            pltpu.make_async_copy(update_buf.at[m, :, cols], update.at[:, cols], out_sems.at[m, 0]).start()
            residue_buf[m, :, cols] = (work[m, :, cols] - approx).astype(BF16)
            pltpu.make_async_copy(residue_buf.at[m, :, cols], residue.at[0, :, cols], out_sems.at[m, 1]).start()

        loop(SLICES, part)
    for m in range(2):
        total_wait(columns.at[m], column_sems.at[m])
        total_wait(update_buf.at[m], out_sems.at[m, 0])
        total_wait(residue_buf.at[m], out_sems.at[m, 1])


def finish(columns, left, work):
    return pl.pallas_call(
        finish_kernel,
        out_shape=(
            jax.ShapeDtypeStruct((RANK, COLS), F32),
            jax.ShapeDtypeStruct((RANK, COLS), F32),
            jax.ShapeDtypeStruct((ROWS, COLS), BF16),
            jax.ShapeDtypeStruct((ROWS, COLS), BF16),
            jax.ShapeDtypeStruct((1, ROWS, COLS), BF16),
            jax.ShapeDtypeStruct((1, ROWS, COLS), BF16),
        ),
        in_specs=[pl.BlockSpec(memory_space=pltpu.VMEM)] * 3,
        out_specs=[pl.BlockSpec(memory_space=pltpu.HBM)] * 6,
        scratch_shapes=[
            pltpu.VMEM((2, ROWS, COLS), BF16),
            pltpu.VMEM((2, ROWS, COLS), BF16),
            pltpu.SemaphoreType.DMA((2,)),
            pltpu.SemaphoreType.DMA((2, 2)),
        ],
        compiler_params=pltpu.CompilerParams(vmem_limit_bytes=24 << 20),
    )(columns, left, work)


def shards(gate_grad, gate_scale, gate_error, gate_prior, up_grad, up_scale, up_error, up_prior):
    args = (
        gate_grad, gate_scale.transpose(0, 2, 1), gate_error, gate_prior.T,
        up_grad, up_scale.transpose(0, 2, 1), up_error, up_prior.T,
    )
    columns, left, work = exchange(*(pltpu.with_memory_space_constraint(a, pltpu.HBM) for a in args))
    columns0, columns1, update0, update1, residue0, residue1 = finish(columns, left, work)
    return (columns0.T, columns1.T, update0, update1, residue0, residue1)


def solution(mesh):
    in_specs = (
        P("dp", "tensor", None),
        P("dp", "tensor", None),
        P("dp", "tensor", None),
        P(),
        P("dp", "tensor", None),
        P("dp", "tensor", None),
        P("dp", "tensor", None),
        P(),
    )
    out_specs = (
        P(),
        P(),
        P("tensor", None),
        P("tensor", None),
        P("dp", "tensor", None),
        P("dp", "tensor", None),
    )
    return jax.shard_map(shards, mesh=mesh, in_specs=in_specs, out_specs=out_specs, check_vma=False)
```

```python
import jax
import jax.numpy as jnp
from jax import lax
from jax.experimental import pallas as pl
from jax.experimental.pallas import tpu as pltpu
from jax.sharding import PartitionSpec as P

MESH = pl.DeviceIdType.MESH
F32 = jnp.float32
BF16 = jnp.bfloat16

ROWS = 128
COLS = 4096
RANK = 32
BLOCK = 128
NZ = 8
NXY = 16
PARTS = 4
RANKS = RANK // PARTS
PIECE = COLS // NXY
CHUNKS = 4
WIDTH = COLS // CHUNKS
LOADS = 2
LOAD = COLS // LOADS
SLICES = 8
SLICE = COLS // SLICES

NN = (((1,), (0,)), ((), ()))
NT = (((1,), (1,)), ((), ()))


def split2(a):
    hi = a.astype(BF16)
    lo = (a - hi.astype(F32)).astype(BF16)
    return hi, lo


def split3(a):
    hi = a.astype(BF16)
    rest = a - hi.astype(F32)
    mid = rest.astype(BF16)
    lo = (rest - mid.astype(F32)).astype(BF16)
    return hi, mid, lo


def mm(a, b, dims=NN):
    return lax.dot_general(a, b, dims, preferred_element_type=F32)


def exact(a, b, dims=NN):
    return lax.dot_general(a, b, dims, preferred_element_type=F32, precision=lax.Precision.HIGHEST)


def inverse_factor(gram):
    rows = lax.broadcasted_iota(jnp.int32, (RANK, 1), 0)
    eye = (lax.broadcasted_iota(jnp.int32, (RANK, RANK), 0) == lax.broadcasted_iota(jnp.int32, (RANK, RANK), 1)).astype(F32)
    left, right = gram, eye
    roots = jnp.zeros((RANK, 1), F32)
    for j in range(RANK):
        pivot = left[j : j + 1, j : j + 1]
        roots = jnp.where(rows == j, lax.rsqrt(pivot), roots)
        factor = jnp.where(rows > j, left[:, j : j + 1] / pivot, 0.0)
        left = left - factor * left[j : j + 1, :]
        right = right - factor * right[j : j + 1, :]
    return right * roots


def total_wait(ref, sem):
    pltpu.make_async_copy(ref, ref, sem).wait()


def send(ref, dst, send_sem, recv_sem, peer):
    pltpu.make_async_remote_copy(
        src_ref=ref, dst_ref=dst, send_sem=send_sem, recv_sem=recv_sem, device_id=peer, device_id_type=MESH
    ).start()


def loop(count, body):
    lax.fori_loop(0, count, lambda i, carry: (body(i), carry)[1], 0)


def exchange_kernel(
    g0, s0, e0, p0, g1, s1, e1, p1,
    columns, left, work,
    g_buf, e_buf, s_buf, p_buf, w_pair, u_hi, u_lo,
    f_part, f_pair, f_z, f_all, gram_xy, inverse_ref, basis, summed,
    t_own, t_xy, t_z,
    small_sems, in_sems, one_send, one_recv, w_send, w_recv, fz_send, fz_recv,
    rs_send, rs_recv, tz_send, tz_recv, ag_send, ag_recv, cp_send, cp_recv,
):
    dp = lax.axis_index("dp")
    me = lax.axis_index("tensor")
    z, c = dp // 2, dp % 2
    x, y = me // 4, me % 4
    other = 1 - c
    sibling = {"dp": z * 2 + other, "tensor": me}

    def z_peer(i):
        return {"dp": lax.rem(z + 1 + lax.rem(i + 3, NZ - 1), NZ) * 2 + c, "tensor": me}

    def xy_index(i):
        k = 1 + lax.rem(i + 9, NXY - 1)
        return lax.rem(x + k // 4, 4) * 4 + lax.rem(y + k % 4, 4)

    def xy_peer(i):
        return {"dp": dp, "tensor": xy_index(i)}

    refs = ((g0, s0, e0, p0), (g1, s1, e1, p1))
    for m, (g, sc, e, p) in enumerate(refs):
        pltpu.make_async_copy(sc.at[0], s_buf.at[m], small_sems.at[m, 0]).start()
        pltpu.make_async_copy(p, p_buf.at[m], small_sems.at[m, 1]).start()
    for k in range(LOADS):
        cols = pl.ds(k * LOAD, LOAD)
        for m, (g, sc, e, p) in enumerate(refs):
            pltpu.make_async_copy(g.at[0, :, cols], g_buf.at[m, :, cols], in_sems.at[m, k, 0]).start()
            pltpu.make_async_copy(e.at[0, :, cols], e_buf.at[m, :, cols], in_sems.at[m, k, 1]).start()

    barrier = pltpu.get_barrier_semaphore()

    def greet(peer):
        pl.semaphore_signal(barrier, inc=1, device_id=peer, device_id_type=MESH)

    loop(NXY - 1, lambda i: greet(xy_peer(i)))
    loop(NZ - 1, lambda i: greet(z_peer(i)))
    greet(sibling)
    summed[...] = jnp.zeros_like(summed)

    for m in range(2):
        total_wait(s_buf.at[m], small_sems.at[m, 0])
        total_wait(p_buf.at[m], small_sems.at[m, 1])

    def partial(k, totals):
        cols = pl.ds(pl.multiple_of(k * LOAD, LOAD), LOAD)
        count = LOAD // BLOCK
        for m in range(2):
            total_wait(g_buf.at[m, :, cols], in_sems.at[m, k, 0])
            total_wait(e_buf.at[m, :, cols], in_sems.at[m, k, 1])
        result = []
        zero = jnp.zeros((ROWS, BLOCK), BF16)
        for m in range(2):
            total = totals[m]
            scale = s_buf[m, pl.ds(pl.multiple_of(k * count, count), count), :].T
            for b in range(0, count, 2):
                at = pl.ds(pl.multiple_of(k * LOAD + b * BLOCK, 2 * BLOCK), 2 * BLOCK)
                hi, mid, lo = split3(p_buf[m, :, at])
                prior = jnp.concatenate([hi, mid, lo, jnp.zeros_like(hi)], 0)
                even = jnp.concatenate([prior[:, :BLOCK], zero], 1)
                odd = jnp.concatenate([zero, prior[:, BLOCK:]], 1)
                both = jnp.concatenate([g_buf[m, :, at], e_buf[m, :, at]], 0)
                out = mm(both, jnp.concatenate([even, odd], 0), NT)
                scaled = out[:ROWS, :128] * scale[:, b : b + 1] + out[:ROWS, 128:] * scale[:, b + 1 : b + 2]
                total = total + (scaled + (out[ROWS:, :128] + out[ROWS:, 128:]))
            result.append(total)
        return tuple(result)

    start = jnp.zeros((ROWS, 128), F32)
    totals = lax.fori_loop(0, LOADS, partial, (start, start))
    for m in range(2):
        total = totals[m]
        factor = total[:, :RANK] + (total[:, RANK : 2 * RANK] + total[:, 2 * RANK : 3 * RANK])
        f_part[m] = factor.T

    pl.semaphore_wait(barrier, 1 + (NZ - 1) + (NXY - 1))

    send(f_part.at[other], f_pair, one_send.at[0], one_recv.at[0], sibling)

    def values(m, k):
        count = WIDTH // BLOCK
        scale = s_buf[m, pl.ds(pl.multiple_of(k * count, count), count), :].T
        for b in range(count):
            at = pl.ds(pl.multiple_of(k * WIDTH + b * BLOCK, BLOCK), BLOCK)
            work[m, :, at] = g_buf[m, :, at].astype(F32) * scale[:, b : b + 1] + e_buf[m, :, at].astype(F32)

    def chunk_of(k):
        return pl.ds(pl.multiple_of(k * WIDTH, WIDTH), WIDTH)

    def give(k):
        values(other, k)
        cols = chunk_of(k)
        send(work.at[other, :, cols], w_pair.at[:, cols], w_send.at[k], w_recv.at[k], sibling)

    loop(CHUNKS, give)
    total_wait(f_pair, one_recv.at[0])
    for q in range(PARTS):
        rows = slice(q * RANKS, (q + 1) * RANKS)
        f_z[q, z] = f_part[c, rows] + f_pair[rows]

    def spread(q):
        loop(NZ - 1, lambda i: send(f_z.at[q, z], f_z.at[q, z], fz_send.at[q], fz_recv.at[q], z_peer(i)))

    loop(PARTS, spread)

    loop(CHUNKS, lambda k: values(c, k))

    def take(k):
        cols = chunk_of(k)
        total_wait(w_pair.at[:, cols], w_recv.at[k])
        hi, lo = split2(work[c, :, cols] + w_pair[:, cols])
        u_hi[:, cols] = hi
        u_lo[:, cols] = lo

    loop(CHUNKS, take)
    total_wait(f_pair, one_send.at[0])
    loop(CHUNKS, lambda k: total_wait(w_pair.at[:, chunk_of(k)], w_send.at[k]))

    def flow(q):
        total_wait(f_z.at[q, pl.ds(0, NZ - 1)], fz_recv.at[q])
        total = f_z[q, 0]
        for k in range(1, NZ):
            total = total + f_z[q, k]
        f_all[q] = total
        hi, lo = split2(total)
        lhs = jnp.concatenate([jnp.concatenate([hi, hi], 1), jnp.concatenate([lo, jnp.zeros_like(lo)], 1)], 0)
        both = mm(lhs, jnp.concatenate([u_hi[...], u_lo[...]], 0))
        t_own[q] = both[:RANKS] + both[RANKS:]

        def scatter(j):
            cols = pl.ds(pl.multiple_of(xy_index(j) * PIECE, PIECE), PIECE)
            send(t_own.at[q, :, cols], t_xy.at[q, me], rs_send.at[q], rs_recv.at[q], xy_peer(j))

        loop(NXY - 1, scatter)
        t_xy[q, me] = t_own[q, :, pl.ds(pl.multiple_of(me * PIECE, PIECE), PIECE)]

    loop(PARTS, flow)

    mine = jnp.concatenate([f_all[q] for q in range(PARTS)], 0)
    gram = exact(mine, mine, NT)
    gram_xy[me] = jnp.concatenate([gram[q * RANKS : (q + 1) * RANKS] for q in range(PARTS)], 1)
    loop(NXY - 1, lambda j: send(gram_xy.at[me], gram_xy.at[me], one_send.at[1], one_recv.at[1], xy_peer(j)))

    def middle(q):
        total_wait(t_xy.at[q, pl.ds(0, NXY - 1)], rs_recv.at[q])
        total = t_xy[q, 0]
        for k in range(1, NXY):
            total = total + t_xy[q, k]
        t_z[q, z] = total
        loop(NZ - 1, lambda i: send(t_z.at[q, z], t_z.at[q, z], tz_send.at[q], tz_recv.at[q], z_peer(i)))

    loop(PARTS, middle)
    loop(PARTS, lambda q: total_wait(f_z.at[q, pl.ds(0, NZ - 1)], fz_send.at[q]))
    loop(PARTS, lambda q: total_wait(t_xy.at[q, pl.ds(0, NXY - 1)], rs_send.at[q]))

    total_wait(gram_xy.at[pl.ds(0, NXY - 1)], one_recv.at[1])
    packed = gram_xy[0]
    for k in range(1, NXY):
        packed = packed + gram_xy[k]
    gram = jnp.concatenate([packed[:, q * RANK : (q + 1) * RANK] for q in range(PARTS)], 0)
    inverse = inverse_factor(gram)
    basis[c] = exact(inverse, mine)
    send(basis.at[c], basis.at[c], one_send.at[2], one_recv.at[2], sibling)
    hi, mid, lo = split3(inverse)
    stacked = jnp.concatenate([hi, hi, mid, hi, mid, lo], 1)
    for q in range(PARTS):
        inverse_ref[q] = stacked[q * RANKS : (q + 1) * RANKS].astype(F32)

    own_cols = pl.ds(pl.multiple_of(me * PIECE, PIECE), PIECE)

    def gather(q):
        total_wait(t_z.at[q, pl.ds(0, NZ - 1)], tz_recv.at[q])
        total = t_z[q, 0]
        for k in range(1, NZ):
            total = total + t_z[q, k]
        rows = pl.ds(pl.multiple_of(q * RANKS, RANKS), RANKS)
        summed[rows, :] = total
        hi, mid, lo = split3(summed[...])
        rhs = jnp.concatenate([hi, mid, hi, lo, mid, hi], 0)
        columns[c, rows, own_cols] = mm(inverse_ref[q].astype(BF16), rhs) * (1.0 / 16.0)
        piece = columns.at[c, rows, own_cols]
        loop(NXY - 1, lambda j: send(piece, piece, ag_send.at[q], ag_recv.at[q], xy_peer(j)))

    loop(PARTS, gather)

    total_wait(basis.at[other], one_recv.at[2])
    for m in range(2):
        hi, lo = split2(basis[m].T)
        left[m] = jnp.concatenate([hi, hi, lo], 1)

    total_wait(gram_xy.at[pl.ds(0, NXY - 1)], one_send.at[1])
    total_wait(basis.at[c], one_send.at[2])
    loop(PARTS, lambda q: total_wait(t_z.at[q, pl.ds(0, NZ - 1)], tz_send.at[q]))

    def hand(q):
        total_wait(t_xy.at[q, pl.ds(0, NXY - 1)], ag_recv.at[q])
        rows = pl.ds(pl.multiple_of(q * RANKS, RANKS), RANKS)
        send(columns.at[c, rows], columns.at[c, rows], cp_send.at[q], cp_recv.at[q], sibling)
        total_wait(t_xy.at[q, pl.ds(0, NXY - 1)], ag_send.at[q])

    loop(PARTS, hand)

    def drain(q):
        rows = pl.ds(pl.multiple_of(q * RANKS, RANKS), RANKS)
        total_wait(columns.at[c, rows], cp_recv.at[q])
        total_wait(columns.at[c, rows], cp_send.at[q])

    loop(PARTS, drain)


def exchange(*args):
    vmem, sems = pltpu.VMEM, pltpu.SemaphoreType.DMA
    return pl.pallas_call(
        exchange_kernel,
        out_shape=(
            jax.ShapeDtypeStruct((2, RANK, COLS), F32),
            jax.ShapeDtypeStruct((2, ROWS, 3 * RANK), BF16),
            jax.ShapeDtypeStruct((2, ROWS, COLS), F32),
        ),
        in_specs=[pl.BlockSpec(memory_space=pltpu.HBM)] * 8,
        out_specs=[pl.BlockSpec(memory_space=pltpu.VMEM)] * 3,
        scratch_shapes=[
            vmem((2, ROWS, COLS), BF16),
            vmem((2, ROWS, COLS), BF16),
            vmem((2, COLS // BLOCK, ROWS), F32),
            vmem((2, RANK, COLS), F32),
            vmem((ROWS, COLS), F32),
            vmem((ROWS, COLS), BF16),
            vmem((ROWS, COLS), BF16),
            vmem((2, RANK, ROWS), F32),
            vmem((RANK, ROWS), F32),
            vmem((PARTS, NZ, RANKS, ROWS), F32),
            vmem((PARTS, RANKS, ROWS), F32),
            vmem((NXY, RANKS, RANK * PARTS), F32),
            vmem((PARTS, RANKS, 6 * RANK), F32),
            vmem((2, RANK, ROWS), F32),
            vmem((RANK, PIECE), F32),
            vmem((PARTS, RANKS, COLS), F32),
            vmem((PARTS, NXY, RANKS, PIECE), F32),
            vmem((PARTS, NZ, RANKS, PIECE), F32),
            sems((2, 2)),
            sems((2, LOADS, 2)),
            sems((3,)),
            sems((3,)),
            sems((CHUNKS,)),
            sems((CHUNKS,)),
        ]
        + [sems((PARTS,))] * 10,
        compiler_params=pltpu.CompilerParams(collective_id=0, has_side_effects=True, vmem_limit_bytes=28 << 20),
        cost_estimate=pl.CostEstimate(flops=1 << 30, bytes_accessed=8 << 20, transcendentals=0),
    )(*args)


def finish_kernel(
    columns, left, work,
    out0, out1, update0, update1, residue0, residue1,
    update_buf, residue_buf, column_sems, out_sems,
):
    outs = (out0, out1)
    for m in range(2):
        pltpu.make_async_copy(columns.at[m], outs[m], column_sems.at[m]).start()
    for m, (update, residue) in enumerate(((update0, residue0), (update1, residue1))):

        def part(k):
            cols = pl.ds(pl.multiple_of(k * SLICE, SLICE), SLICE)
            hi, lo = split2(columns[m, :, cols])
            approx = mm(left[m], jnp.concatenate([hi, lo, hi], 0))
            update_buf[m, :, cols] = approx.astype(BF16)
            pltpu.make_async_copy(update_buf.at[m, :, cols], update.at[:, cols], out_sems.at[m, 0]).start()
            residue_buf[m, :, cols] = (work[m, :, cols] - approx).astype(BF16)
            pltpu.make_async_copy(residue_buf.at[m, :, cols], residue.at[0, :, cols], out_sems.at[m, 1]).start()

        loop(SLICES, part)
    for m in range(2):
        total_wait(columns.at[m], column_sems.at[m])
        total_wait(update_buf.at[m], out_sems.at[m, 0])
        total_wait(residue_buf.at[m], out_sems.at[m, 1])


def finish(columns, left, work):
    return pl.pallas_call(
        finish_kernel,
        out_shape=(
            jax.ShapeDtypeStruct((RANK, COLS), F32),
            jax.ShapeDtypeStruct((RANK, COLS), F32),
            jax.ShapeDtypeStruct((ROWS, COLS), BF16),
            jax.ShapeDtypeStruct((ROWS, COLS), BF16),
            jax.ShapeDtypeStruct((1, ROWS, COLS), BF16),
            jax.ShapeDtypeStruct((1, ROWS, COLS), BF16),
        ),
        in_specs=[pl.BlockSpec(memory_space=pltpu.VMEM)] * 3,
        out_specs=[pl.BlockSpec(memory_space=pltpu.HBM)] * 6,
        scratch_shapes=[
            pltpu.VMEM((2, ROWS, COLS), BF16),
            pltpu.VMEM((2, ROWS, COLS), BF16),
            pltpu.SemaphoreType.DMA((2,)),
            pltpu.SemaphoreType.DMA((2, 2)),
        ],
        compiler_params=pltpu.CompilerParams(vmem_limit_bytes=24 << 20),
    )(columns, left, work)


def shards(gate_grad, gate_scale, gate_error, gate_prior, up_grad, up_scale, up_error, up_prior):
    args = (
        gate_grad, gate_scale.transpose(0, 2, 1), gate_error, gate_prior.T,
        up_grad, up_scale.transpose(0, 2, 1), up_error, up_prior.T,
    )
    columns, left, work = exchange(*(pltpu.with_memory_space_constraint(a, pltpu.HBM) for a in args))
    columns0, columns1, update0, update1, residue0, residue1 = finish(columns, left, work)
    return (columns0.T, columns1.T, update0, update1, residue0, residue1)


def solution(mesh):
    in_specs = (
        P("dp", "tensor", None),
        P("dp", "tensor", None),
        P("dp", "tensor", None),
        P(),
        P("dp", "tensor", None),
        P("dp", "tensor", None),
        P("dp", "tensor", None),
        P(),
    )
    out_specs = (
        P(),
        P(),
        P("tensor", None),
        P("tensor", None),
        P("dp", "tensor", None),
        P("dp", "tensor", None),
    )
    return jax.shard_map(shards, mesh=mesh, in_specs=in_specs, out_specs=out_specs, check_vma=False)
```

```python
import jax
import jax.numpy as jnp
from jax import lax
from jax.experimental import pallas as pl
from jax.experimental.pallas import tpu as pltpu
from jax.sharding import PartitionSpec as P

MESH = pl.DeviceIdType.MESH
F32 = jnp.float32
BF16 = jnp.bfloat16

ROWS = 128
COLS = 4096
RANK = 32
BLOCK = 128
NZ = 8
NXY = 16
PARTS = 4
RANKS = RANK // PARTS
PIECE = COLS // NXY
CHUNKS = 4
WIDTH = COLS // CHUNKS
LOADS = 2
LOAD = COLS // LOADS
SLICES = 4
SLICE = COLS // SLICES

NN = (((1,), (0,)), ((), ()))
NT = (((1,), (1,)), ((), ()))


def split2(a):
    hi = a.astype(BF16)
    lo = (a - hi.astype(F32)).astype(BF16)
    return hi, lo


def split3(a):
    hi = a.astype(BF16)
    rest = a - hi.astype(F32)
    mid = rest.astype(BF16)
    lo = (rest - mid.astype(F32)).astype(BF16)
    return hi, mid, lo


def mm(a, b, dims=NN):
    return lax.dot_general(a, b, dims, preferred_element_type=F32)


def exact(a, b, dims=NN):
    return lax.dot_general(a, b, dims, preferred_element_type=F32, precision=lax.Precision.HIGHEST)


def inverse_factor(gram):
    rows = lax.broadcasted_iota(jnp.int32, (RANK, 1), 0)
    eye = (lax.broadcasted_iota(jnp.int32, (RANK, RANK), 0) == lax.broadcasted_iota(jnp.int32, (RANK, RANK), 1)).astype(F32)
    left, right = gram, eye
    roots = jnp.zeros((RANK, 1), F32)
    for j in range(RANK):
        pivot = left[j : j + 1, j : j + 1]
        roots = jnp.where(rows == j, lax.rsqrt(pivot), roots)
        factor = jnp.where(rows > j, left[:, j : j + 1] / pivot, 0.0)
        left = left - factor * left[j : j + 1, :]
        right = right - factor * right[j : j + 1, :]
    return right * roots


def total_wait(ref, sem):
    pltpu.make_async_copy(ref, ref, sem).wait()


def send(ref, dst, send_sem, recv_sem, peer):
    pltpu.make_async_remote_copy(
        src_ref=ref, dst_ref=dst, send_sem=send_sem, recv_sem=recv_sem, device_id=peer, device_id_type=MESH
    ).start()


def loop(count, body):
    if count in (NXY - 1, NZ - 1):
        for i in range(count):
            body(i)
        return

    lax.fori_loop(0, count, lambda i, carry: (body(i), carry)[1], 0)


def exchange_kernel(
    g0, s0, e0, p0, g1, s1, e1, p1,
    sums, left, work,
    g_buf, e_buf, s_buf, p_buf, w_pair, u_hi, u_lo,
    f_part, f_pair, f_z, f_all, gram_xy, solved,
    t_own, t_xy, t_z,
    small_sems, in_sems, one_send, one_recv, w_send, w_recv, fz_send, fz_recv,
    rs_send, rs_recv, tz_send, tz_recv, ag_send, ag_recv, cp_send, cp_recv, last_send, last_recv,
):
    dp = lax.axis_index("dp")
    me = lax.axis_index("tensor")
    z, c = dp // 2, dp % 2
    x, y = me // 4, me % 4
    other = 1 - c
    sibling = {"dp": z * 2 + other, "tensor": me}

    def z_peer(i):
        return {"dp": lax.rem(z + 1 + ((i + 3) % (NZ - 1)), NZ) * 2 + c, "tensor": me}

    def xy_index(i):
        k = 1 + ((i + 9) % (NXY - 1))
        return lax.rem(x + k // 4, 4) * 4 + lax.rem(y + k % 4, 4)

    def xy_peer(i):
        return {"dp": dp, "tensor": xy_index(i)}

    def xy_cross(i):
        return {"dp": z * 2 + other, "tensor": xy_index(i)}

    refs = ((g0, s0, e0, p0), (g1, s1, e1, p1))
    for m, (g, sc, e, p) in enumerate(refs):
        pltpu.make_async_copy(sc.at[0], s_buf.at[m], small_sems.at[m, 0]).start()
        pltpu.make_async_copy(p, p_buf.at[m], small_sems.at[m, 1]).start()
    for k in range(LOADS):
        cols = pl.ds(k * LOAD, LOAD)
        for m, (g, sc, e, p) in enumerate(refs):
            pltpu.make_async_copy(g.at[0, :, cols], g_buf.at[m, :, cols], in_sems.at[m, k, 0]).start()
            pltpu.make_async_copy(e.at[0, :, cols], e_buf.at[m, :, cols], in_sems.at[m, k, 1]).start()

    barrier = pltpu.get_barrier_semaphore()

    def greet(peer):
        pl.semaphore_signal(barrier, inc=1, device_id=peer, device_id_type=MESH)

    loop(NXY - 1, lambda i: greet(xy_peer(i)))
    loop(NZ - 1, lambda i: greet(z_peer(i)))
    loop(NXY - 1, lambda i: greet(xy_cross(i)))
    greet(sibling)

    for m in range(2):
        total_wait(s_buf.at[m], small_sems.at[m, 0])
        total_wait(p_buf.at[m], small_sems.at[m, 1])

    def partial(k, totals):
        cols = pl.ds(pl.multiple_of(k * LOAD, LOAD), LOAD)
        count = LOAD // BLOCK
        for m in range(2):
            total_wait(g_buf.at[m, :, cols], in_sems.at[m, k, 0])
            total_wait(e_buf.at[m, :, cols], in_sems.at[m, k, 1])
        result = []
        zero = jnp.zeros((ROWS, BLOCK), BF16)
        for m in range(2):
            total = totals[m]
            scale = s_buf[m, pl.ds(pl.multiple_of(k * count, count), count), :].T
            for b in range(0, count, 2):
                at = pl.ds(pl.multiple_of(k * LOAD + b * BLOCK, 2 * BLOCK), 2 * BLOCK)
                hi, mid, lo = split3(p_buf[m, :, at])
                prior = jnp.concatenate([hi, mid, lo, jnp.zeros_like(hi)], 0)
                even = jnp.concatenate([prior[:, :BLOCK], zero], 1)
                odd = jnp.concatenate([zero, prior[:, BLOCK:]], 1)
                both = jnp.concatenate([g_buf[m, :, at], e_buf[m, :, at]], 0)
                out = mm(both, jnp.concatenate([even, odd], 0), NT)
                scaled = out[:ROWS, :128] * scale[:, b : b + 1] + out[:ROWS, 128:] * scale[:, b + 1 : b + 2]
                total = total + (scaled + (out[ROWS:, :128] + out[ROWS:, 128:]))
            result.append(total)
        return tuple(result)

    start = jnp.zeros((ROWS, 128), F32)
    totals = lax.fori_loop(0, LOADS, partial, (start, start))
    for m in range(2):
        total = totals[m]
        factor = total[:, :RANK] + (total[:, RANK : 2 * RANK] + total[:, 2 * RANK : 3 * RANK])
        f_part[m] = factor.T

    pl.semaphore_wait(barrier, 1 + (NZ - 1) + 2 * (NXY - 1))

    send(f_part.at[other], f_pair, one_send.at[0], one_recv.at[0], sibling)

    def values(m, k):
        count = WIDTH // BLOCK
        scale = s_buf[m, pl.ds(pl.multiple_of(k * count, count), count), :].T
        for b in range(count):
            at = pl.ds(pl.multiple_of(k * WIDTH + b * BLOCK, BLOCK), BLOCK)
            work[m, :, at] = g_buf[m, :, at].astype(F32) * scale[:, b : b + 1] + e_buf[m, :, at].astype(F32)

    def chunk_of(k):
        return pl.ds(pl.multiple_of(k * WIDTH, WIDTH), WIDTH)

    def give(k):
        values(other, k)
        cols = chunk_of(k)
        send(work.at[other, :, cols], w_pair.at[:, cols], w_send.at[k], w_recv.at[k], sibling)

    lax.fori_loop(0, CHUNKS // 2, lambda k, carry: (give(k), carry)[1], 0)
    total_wait(f_pair, one_recv.at[0])
    for q in range(PARTS):
        rows = slice(q * RANKS, (q + 1) * RANKS)
        f_z[q, z] = f_part[c, rows] + f_pair[rows]

    def spread(q):
        loop(NZ - 1, lambda i: send(f_z.at[q, z], f_z.at[q, z], fz_send.at[q], fz_recv.at[q], z_peer(i)))

    loop(PARTS, spread)

    lax.fori_loop(CHUNKS // 2, CHUNKS, lambda k, carry: (give(k), carry)[1], 0)
    loop(CHUNKS, lambda k: values(c, k))

    def take(k):
        cols = chunk_of(k)
        total_wait(w_pair.at[:, cols], w_recv.at[k])
        hi, lo = split2(work[c, :, cols] + w_pair[:, cols])
        u_hi[:, cols] = hi
        u_lo[:, cols] = lo

    loop(CHUNKS, take)
    total_wait(f_pair, one_send.at[0])
    loop(CHUNKS, lambda k: total_wait(w_pair.at[:, chunk_of(k)], w_send.at[k]))

    def flow(q):
        total_wait(f_z.at[q, pl.ds(0, NZ - 1)], fz_recv.at[q])
        total = f_z[q, 0]
        for k in range(1, NZ):
            total = total + f_z[q, k]
        f_all[q] = total
        hi, lo = split2(total)
        lhs = jnp.concatenate([jnp.concatenate([hi, hi], 1), jnp.concatenate([lo, jnp.zeros_like(lo)], 1)], 0)
        both = mm(lhs, jnp.concatenate([u_hi[...], u_lo[...]], 0))
        t_own[q] = both[:RANKS] + both[RANKS:]

        def scatter(j):
            cols = pl.ds(pl.multiple_of(xy_index(j) * PIECE, PIECE), PIECE)
            send(t_own.at[q, :, cols], t_xy.at[q, me], rs_send.at[q], rs_recv.at[q], xy_peer(j))

        loop(NXY - 1, scatter)
        t_xy[q, me] = t_own[q, :, pl.ds(pl.multiple_of(me * PIECE, PIECE), PIECE)]

    loop(PARTS, flow)

    mine = jnp.concatenate([f_all[q] for q in range(PARTS)], 0)
    gram = exact(mine, mine, NT)
    gram_xy[me] = jnp.concatenate([gram[q * RANKS : (q + 1) * RANKS] for q in range(PARTS)], 1)
    loop(NXY - 1, lambda j: send(gram_xy.at[me], gram_xy.at[me], one_send.at[1], one_recv.at[1], xy_peer(j)))

    def middle(q):
        total_wait(t_xy.at[q, pl.ds(0, NXY - 1)], rs_recv.at[q])
        total = t_xy[q, 0]
        for k in range(1, NXY):
            total = total + t_xy[q, k]
        t_z[q, z] = total
        loop(NZ - 1, lambda i: send(t_z.at[q, z], t_z.at[q, z], tz_send.at[q], tz_recv.at[q], z_peer(i)))

    loop(PARTS, middle)
    loop(PARTS, lambda q: total_wait(f_z.at[q, pl.ds(0, NZ - 1)], fz_send.at[q]))
    loop(PARTS, lambda q: total_wait(t_xy.at[q, pl.ds(0, NXY - 1)], rs_send.at[q]))

    own_cols = pl.ds(pl.multiple_of(me * PIECE, PIECE), PIECE)

    def collect(q):
        total_wait(t_z.at[q, pl.ds(0, NZ - 1)], tz_recv.at[q])
        total = t_z[q, 0]
        for k in range(1, NZ):
            total = total + t_z[q, k]
        rows = pl.ds(q * RANKS if isinstance(q, int) else pl.multiple_of(q * RANKS, RANKS), RANKS)
        sums[c, rows, own_cols] = total
        return sums.at[c, rows, own_cols]

    def gather(q):
        piece = collect(q)
        loop(NXY - 1, lambda j: send(piece, piece, ag_send.at[q], ag_recv.at[q], xy_peer(j)))

    loop(PARTS - 1, gather)
    final = PARTS - 1
    piece = collect(final)

    def both_cores(j):
        send(piece, piece, ag_send.at[final], ag_recv.at[final], xy_peer(j))
        send(piece, piece, last_send.at[0], last_recv.at[0], xy_cross(j))

    loop(NXY - 1, both_cores)
    send(piece, piece, last_send.at[0], last_recv.at[0], sibling)

    total_wait(gram_xy.at[pl.ds(0, NXY - 1)], one_recv.at[1])
    packed = gram_xy[0]
    for k in range(1, NXY):
        packed = packed + gram_xy[k]
    gram = jnp.concatenate([packed[:, q * RANK : (q + 1) * RANK] for q in range(PARTS)], 0)
    inverse = inverse_factor(gram)
    basis = exact(inverse, mine)
    solved[c, 0] = exact(inverse.T, basis)
    solved[c, 1] = jnp.concatenate([inverse.T, jnp.zeros((RANK, ROWS - RANK), F32)], 1)
    send(solved.at[c], solved.at[c], one_send.at[2], one_recv.at[2], sibling)

    def hand(q):
        total_wait(t_xy.at[q, pl.ds(0, NXY - 1)], ag_recv.at[q])
        rows = pl.ds(pl.multiple_of(q * RANKS, RANKS), RANKS)
        send(sums.at[c, rows], sums.at[c, rows], cp_send.at[q], cp_recv.at[q], sibling)

    loop(PARTS - 1, hand)

    total_wait(solved.at[other], one_recv.at[2])
    for m in range(2):
        both = jnp.concatenate([solved[m, 0].T, solved[m, 1].T[:RANK]], 0) * (1.0 / 16.0)
        hi, mid, lo = split3(both)
        left[m] = jnp.concatenate([hi, hi, mid, hi, mid, lo], 1)

    total_wait(gram_xy.at[pl.ds(0, NXY - 1)], one_send.at[1])
    total_wait(solved.at[c], one_send.at[2])
    loop(PARTS, lambda q: total_wait(t_z.at[q, pl.ds(0, NZ - 1)], tz_send.at[q]))

    def drain(q):
        rows = pl.ds(pl.multiple_of(q * RANKS, RANKS), RANKS)
        total_wait(sums.at[c, rows], cp_recv.at[q])
        total_wait(sums.at[c, rows], cp_send.at[q])

    loop(PARTS - 1, drain)
    loop(PARTS, lambda q: total_wait(t_xy.at[q, pl.ds(0, NXY - 1)], ag_send.at[q]))
    total_wait(t_xy.at[0], last_send.at[0])
    total_wait(t_xy.at[0, pl.ds(0, NXY - 1)], ag_recv.at[final])
    total_wait(t_xy.at[0], last_recv.at[0])


def exchange(*args):
    vmem, sems = pltpu.VMEM, pltpu.SemaphoreType.DMA
    return pl.pallas_call(
        exchange_kernel,
        out_shape=(
            jax.ShapeDtypeStruct((2, RANK, COLS), F32),
            jax.ShapeDtypeStruct((2, ROWS + RANK, 6 * RANK), BF16),
            jax.ShapeDtypeStruct((2, ROWS, COLS), F32),
        ),
        in_specs=[pl.BlockSpec(memory_space=pltpu.HBM)] * 8,
        out_specs=[pl.BlockSpec(memory_space=pltpu.VMEM)] * 3,
        scratch_shapes=[
            vmem((2, ROWS, COLS), BF16),
            vmem((2, ROWS, COLS), BF16),
            vmem((2, COLS // BLOCK, ROWS), F32),
            vmem((2, RANK, COLS), F32),
            vmem((ROWS, COLS), F32),
            vmem((ROWS, COLS), BF16),
            vmem((ROWS, COLS), BF16),
            vmem((2, RANK, ROWS), F32),
            vmem((RANK, ROWS), F32),
            vmem((PARTS, NZ, RANKS, ROWS), F32),
            vmem((PARTS, RANKS, ROWS), F32),
            vmem((NXY, RANKS, RANK * PARTS), F32),
            vmem((2, 2, RANK, ROWS), F32),
            vmem((PARTS, RANKS, COLS), F32),
            vmem((PARTS, NXY, RANKS, PIECE), F32),
            vmem((PARTS, NZ, RANKS, PIECE), F32),
            sems((2, 2)),
            sems((2, LOADS, 2)),
            sems((3,)),
            sems((3,)),
            sems((CHUNKS,)),
            sems((CHUNKS,)),
        ]
        + [sems((PARTS,))] * 10
        + [sems((1,))] * 2,
        compiler_params=pltpu.CompilerParams(collective_id=0, has_side_effects=True, vmem_limit_bytes=28 << 20),
        cost_estimate=pl.CostEstimate(flops=1 << 30, bytes_accessed=8 << 20, transcendentals=0),
    )(*args)


def finish_kernel(
    sums, left, work,
    out0, out1, update0, update1, residue0, residue1,
    out_buf, update_buf, residue_buf, out_sems,
):
    outputs = ((out0, update0, residue0), (out1, update1, residue1))

    def part(k):
        cols = pl.ds(pl.multiple_of(k * SLICE, SLICE), SLICE)
        for m, (out, update, residue) in enumerate(outputs):
            hi, mid, lo = split3(sums[m, :, cols])
            both = mm(left[m], jnp.concatenate([hi, mid, hi, lo, mid, hi], 0))
            approx = both[:ROWS]
            update_buf[m, :, cols] = approx.astype(BF16)
            residue_buf[m, :, cols] = (work[m, :, cols] - approx).astype(BF16)
            out_buf[m, :, cols] = both[ROWS:]
            pltpu.make_async_copy(update_buf.at[m, :, cols], update.at[:, cols], out_sems.at[m, 0]).start()
            pltpu.make_async_copy(residue_buf.at[m, :, cols], residue.at[0, :, cols], out_sems.at[m, 1]).start()
            pltpu.make_async_copy(out_buf.at[m, :, cols], out.at[:, cols], out_sems.at[m, 2]).start()

    loop(SLICES, part)
    for m in range(2):
        total_wait(update_buf.at[m], out_sems.at[m, 0])
        total_wait(residue_buf.at[m], out_sems.at[m, 1])
        total_wait(out_buf.at[m], out_sems.at[m, 2])


def finish(sums, left, work):
    return pl.pallas_call(
        finish_kernel,
        out_shape=(
            jax.ShapeDtypeStruct((RANK, COLS), F32),
            jax.ShapeDtypeStruct((RANK, COLS), F32),
            jax.ShapeDtypeStruct((ROWS, COLS), BF16),
            jax.ShapeDtypeStruct((ROWS, COLS), BF16),
            jax.ShapeDtypeStruct((1, ROWS, COLS), BF16),
            jax.ShapeDtypeStruct((1, ROWS, COLS), BF16),
        ),
        in_specs=[pl.BlockSpec(memory_space=pltpu.VMEM)] * 3,
        out_specs=[pl.BlockSpec(memory_space=pltpu.HBM)] * 6,
        scratch_shapes=[
            pltpu.VMEM((2, RANK, COLS), F32),
            pltpu.VMEM((2, ROWS, COLS), BF16),
            pltpu.VMEM((2, ROWS, COLS), BF16),
            pltpu.SemaphoreType.DMA((2, 3)),
        ],
        compiler_params=pltpu.CompilerParams(vmem_limit_bytes=24 << 20),
    )(sums, left, work)


def shards(gate_grad, gate_scale, gate_error, gate_prior, up_grad, up_scale, up_error, up_prior):
    args = (
        gate_grad, gate_scale.transpose(0, 2, 1), gate_error, gate_prior.T,
        up_grad, up_scale.transpose(0, 2, 1), up_error, up_prior.T,
    )
    sums, left, work = exchange(*(pltpu.with_memory_space_constraint(a, pltpu.HBM) for a in args))
    columns0, columns1, update0, update1, residue0, residue1 = finish(sums, left, work)
    return (columns0.T, columns1.T, update0, update1, residue0, residue1)


def solution(mesh):
    in_specs = (
        P("dp", "tensor", None),
        P("dp", "tensor", None),
        P("dp", "tensor", None),
        P(),
        P("dp", "tensor", None),
        P("dp", "tensor", None),
        P("dp", "tensor", None),
        P(),
    )
    out_specs = (
        P(),
        P(),
        P("tensor", None),
        P("tensor", None),
        P("dp", "tensor", None),
        P("dp", "tensor", None),
    )
    return jax.shard_map(shards, mesh=mesh, in_specs=in_specs, out_specs=out_specs, check_vma=False)
```

```python
import jax
import jax.numpy as jnp
from jax import lax
from jax.experimental import pallas as pl
from jax.experimental.pallas import tpu as pltpu
from jax.sharding import PartitionSpec as P

MESH = pl.DeviceIdType.MESH
F32 = jnp.float32
BF16 = jnp.bfloat16

ROWS = 128
COLS = 4096
RANK = 32
BLOCK = 128
NZ = 8
NXY = 16
PARTS = 4
RANKS = RANK // PARTS
PIECE = COLS // NXY
HALF = PIECE // 2
UNITS = ((0, 0, PIECE), (1, 0, PIECE), (2, 0, PIECE), (3, 0, PIECE))
CHUNKS = 4
WIDTH = COLS // CHUNKS
LOADS = 2
LOAD = COLS // LOADS
SLICES = 8
SLICE = COLS // SLICES

FAR_Z = (4, 3, 5, 2, 6, 1, 7)
FAR_XY = (10, 6, 14, 9, 11, 5, 7, 13, 15, 2, 8, 1, 3, 4, 12)

NN = (((1,), (0,)), ((), ()))
NT = (((1,), (1,)), ((), ()))


def split2(a):
    hi = a.astype(BF16)
    lo = (a - hi.astype(F32)).astype(BF16)
    return hi, lo


def split3(a):
    hi = a.astype(BF16)
    rest = a - hi.astype(F32)
    mid = rest.astype(BF16)
    lo = (rest - mid.astype(F32)).astype(BF16)
    return hi, mid, lo


def mm(a, b, dims=NN):
    return lax.dot_general(a, b, dims, preferred_element_type=F32)


def exact(a, b, dims=NN):
    return lax.dot_general(a, b, dims, preferred_element_type=F32, precision=lax.Precision.HIGHEST)


def inverse_factor(gram):
    rows = lax.broadcasted_iota(jnp.int32, (RANK, 1), 0)
    eye = (lax.broadcasted_iota(jnp.int32, (RANK, RANK), 0) == lax.broadcasted_iota(jnp.int32, (RANK, RANK), 1)).astype(F32)
    left, right = gram, eye
    roots = jnp.zeros((RANK, 1), F32)
    for j in range(RANK):
        pivot = left[j : j + 1, j : j + 1]
        roots = jnp.where(rows == j, lax.rsqrt(pivot), roots)
        factor = jnp.where(rows > j, left[:, j : j + 1] / pivot, 0.0)
        left = left - factor * left[j : j + 1, :]
        right = right - factor * right[j : j + 1, :]
    return right * roots


def total_wait(ref, sem):
    pltpu.make_async_copy(ref, ref, sem).wait()


def send(ref, dst, send_sem, recv_sem, peer):
    pltpu.make_async_remote_copy(
        src_ref=ref, dst_ref=dst, send_sem=send_sem, recv_sem=recv_sem, device_id=peer, device_id_type=MESH
    ).start()


def loop(count, body, unroll=False):
    if count in (NXY - 1, NZ - 1, NZ):
        for i in range(count):
            body(i)
        return

    if unroll:
        for i in range(count):
            body(i)
        return
    lax.fori_loop(0, count, lambda i, carry: (body(i), carry)[1], 0)


def exchange_kernel(
    g0, s0, e0, p0, g1, s1, e1, p1,
    sums, left, work,
    g_buf, e_buf, s_buf, p_buf, w_pair, u_hi, u_lo,
    f_part, f_pair, f_z, f_all, gram_xy, solved,
    t_own, t_xy, t_z,
    small_sems, in_sems, one_send, one_recv, w_send, w_recv, fz_send, fz_recv,
    rs_send, rs_recv, tz_send, tz_recv, ag_send, ag_recv, cp_send, cp_recv, last_send, last_recv,
):
    dp = lax.axis_index("dp")
    me = lax.axis_index("tensor")
    z, c = dp // 2, dp % 2
    x, y = me // 4, me % 4
    other = 1 - c
    sibling = {"dp": z * 2 + other, "tensor": me}

    z_bases = [lax.rem(z + k, NZ) * 2 for k in FAR_Z + (0,)]
    xy_all = [lax.rem(x + k // 4, 4) * 4 + lax.rem(y + k % 4, 4) for k in FAR_XY]

    def z_peer(i):
        return {"dp": z_bases[i] + c, "tensor": me}

    def z_cross(i):
        return {"dp": z_bases[i] + other, "tensor": me}

    def xy_index(i):
        return xy_all[i]

    def xy_peer(i):
        return {"dp": dp, "tensor": xy_index(i)}

    def xy_cross(i):
        return {"dp": z * 2 + other, "tensor": xy_index(i)}

    refs = ((g0, s0, e0, p0), (g1, s1, e1, p1))
    for m, (g, sc, e, p) in enumerate(refs):
        pltpu.make_async_copy(sc.at[0], s_buf.at[m], small_sems.at[m, 0]).start()
        pltpu.make_async_copy(p, p_buf.at[m], small_sems.at[m, 1]).start()

    def fetch(k):
        cols = pl.ds(k * LOAD, LOAD)
        for m, (g, sc, e, p) in enumerate(refs):
            pltpu.make_async_copy(g.at[0, :, cols], g_buf.at[m, :, cols], in_sems.at[m, k, 0]).start()
            pltpu.make_async_copy(e.at[0, :, cols], e_buf.at[m, :, cols], in_sems.at[m, k, 1]).start()

    fetch(0)
    barrier = pltpu.get_barrier_semaphore()

    def greet(peer):
        pl.semaphore_signal(barrier, inc=1, device_id=peer, device_id_type=MESH)

    loop(NZ - 1, lambda i: greet(z_peer(i)))
    greet(sibling)
    loop(NXY - 1, lambda i: greet(xy_peer(i)))
    for k in range(1, LOADS):
        fetch(k)

    for m in range(2):
        total_wait(s_buf.at[m], small_sems.at[m, 0])
        total_wait(p_buf.at[m], small_sems.at[m, 1])

    def partial(k, totals):
        cols = pl.ds(pl.multiple_of(k * LOAD, LOAD), LOAD)
        count = LOAD // BLOCK
        for m in range(2):
            total_wait(g_buf.at[m, :, cols], in_sems.at[m, k, 0])
            total_wait(e_buf.at[m, :, cols], in_sems.at[m, k, 1])
        result = []
        zero = jnp.zeros((ROWS, BLOCK), BF16)
        for m in range(2):
            total = totals[m]
            scale = s_buf[m, pl.ds(pl.multiple_of(k * count, count), count), :].T
            for b in range(0, count, 2):
                at = pl.ds(pl.multiple_of(k * LOAD + b * BLOCK, 2 * BLOCK), 2 * BLOCK)
                hi, mid, lo = split3(p_buf[m, :, at])
                prior = jnp.concatenate([hi, mid, lo, jnp.zeros_like(hi)], 0)
                even = jnp.concatenate([prior[:, :BLOCK], zero], 1)
                odd = jnp.concatenate([zero, prior[:, BLOCK:]], 1)
                both = jnp.concatenate([g_buf[m, :, at], e_buf[m, :, at]], 0)
                out = mm(both, jnp.concatenate([even, odd], 0), NT)
                scaled = out[:ROWS, :128] * scale[:, b : b + 1] + out[:ROWS, 128:] * scale[:, b + 1 : b + 2]
                total = total + (scaled + (out[ROWS:, :128] + out[ROWS:, 128:]))
            result.append(total)
        return tuple(result)

    start = jnp.zeros((ROWS, 128), F32)
    totals = lax.fori_loop(0, LOADS, partial, (start, start))
    for m in range(2):
        total = totals[m]
        factor = total[:, :RANK] + (total[:, RANK : 2 * RANK] + total[:, 2 * RANK : 3 * RANK])
        f_part[m] = factor.T

    pl.semaphore_wait(barrier, NZ + (NXY - 1))

    send(f_part.at[other], f_pair, one_send.at[0], one_recv.at[0], sibling)

    def spread(q):
        f_z[q, z] = f_part[c, q * RANKS : (q + 1) * RANKS] + f_pair[q * RANKS : (q + 1) * RANKS]
        loop(NZ - 1, lambda i: send(f_z.at[q, z], f_z.at[q, z], fz_send.at[q], fz_recv.at[q], z_peer(i)))

    def values(m, k):
        count = WIDTH // BLOCK
        scale = s_buf[m, pl.ds(pl.multiple_of(k * count, count), count), :].T
        for b in range(count):
            at = pl.ds(pl.multiple_of(k * WIDTH + b * BLOCK, BLOCK), BLOCK)
            work[m, :, at] = g_buf[m, :, at].astype(F32) * scale[:, b : b + 1] + e_buf[m, :, at].astype(F32)

    def chunk_of(k):
        return pl.ds(pl.multiple_of(k * WIDTH, WIDTH), WIDTH)

    def give(k):
        values(other, k)
        cols = chunk_of(k)
        send(work.at[other, :, cols], w_pair.at[:, cols], w_send.at[k], w_recv.at[k], sibling)

    give(0)
    give(1)
    total_wait(f_pair, one_recv.at[0])
    for q in range(PARTS):
        spread(q)
    lax.fori_loop(2, CHUNKS, lambda k, carry: (give(k), carry)[1], 0)

    loop(CHUNKS, lambda k: values(c, k))

    def take(k):
        cols = chunk_of(k)
        total_wait(w_pair.at[:, cols], w_recv.at[k])
        hi, lo = split2(work[c, :, cols] + w_pair[:, cols])
        u_hi[:, cols] = hi
        u_lo[:, cols] = lo

    loop(CHUNKS, take)
    total_wait(f_pair, one_send.at[0])
    loop(CHUNKS, lambda k: total_wait(w_pair.at[:, chunk_of(k)], w_send.at[k]))

    def flow(q):
        total_wait(f_z.at[q, pl.ds(0, NZ - 1)], fz_recv.at[q])
        total = f_z[q, 0]
        for k in range(1, NZ):
            total = total + f_z[q, k]
        f_all[q] = total
        hi, lo = split2(total)
        lhs = jnp.concatenate([jnp.concatenate([hi, hi], 1), jnp.concatenate([lo, jnp.zeros_like(lo)], 1)], 0)
        both = mm(lhs, jnp.concatenate([u_hi[...], u_lo[...]], 0))
        t_own[q] = both[:RANKS] + both[RANKS:]

        for u, (chunk, first, width) in enumerate(UNITS):
            if chunk == q:
                for j in range(NXY - 1):
                    cols = pl.ds(pl.multiple_of(first + xy_index(j) * width, width), width)
                    send(t_own.at[q, :, cols], t_xy.at[u, me, :, :width], rs_send.at[u], rs_recv.at[u], xy_peer(j))
                t_xy[u, me, :, :width] = t_own[q, :, pl.ds(pl.multiple_of(first + me * width, width), width)]

    loop(PARTS, flow, True)

    mine = jnp.concatenate([f_all[q] for q in range(PARTS)], 0)
    gram = exact(mine, mine, NT)
    gram_xy[me] = jnp.concatenate([gram[q * RANKS : (q + 1) * RANKS] for q in range(PARTS)], 1)
    loop(NXY - 1, lambda j: send(gram_xy.at[me], gram_xy.at[me], one_send.at[1], one_recv.at[1], xy_peer(j)))

    def middle(q):
        width = UNITS[q][2]
        total_wait(t_xy.at[q, pl.ds(0, NXY - 1), :, :width], rs_recv.at[q])
        total = t_xy[q, 0, :, :width]
        for k in range(1, NXY):
            total = total + t_xy[q, k, :, :width]
        t_z[q, z, :, :width] = total
        piece = t_z.at[q, z, :, :width]
        loop(NZ - 1, lambda i: send(piece, piece, tz_send.at[q], tz_recv.at[q], z_peer(i)))

    loop(len(UNITS), middle, True)
    loop(PARTS, lambda q: total_wait(f_z.at[q, pl.ds(0, NZ - 1)], fz_send.at[q]))
    for u, (chunk, first, width) in enumerate(UNITS):
        total_wait(t_xy.at[u, pl.ds(0, NXY - 1), :, :width], rs_send.at[u])

    def collect(u):
        chunk, first, width = UNITS[u]
        total_wait(t_z.at[u, pl.ds(0, NZ - 1), :, :width], tz_recv.at[u])
        total = t_z[u, 0, :, :width]
        for k in range(1, NZ):
            total = total + t_z[u, k, :, :width]
        rows = pl.ds(chunk * RANKS, RANKS)
        cols = pl.ds(pl.multiple_of(first + me * width, width), width)
        sums[c, rows, cols] = total
        return sums.at[c, rows, cols]

    def gather(u):
        piece = collect(u)
        loop(NXY - 1, lambda j: send(piece, piece, ag_send.at[u], ag_recv.at[u], xy_peer(j)))

    final = len(UNITS) - 1
    loop(final, gather, True)
    piece = collect(final)

    def both_cores(j):
        send(piece, piece, ag_send.at[final], ag_recv.at[final], xy_peer(j))
        send(piece, piece, last_send.at[0], last_recv.at[0], xy_cross(j))

    loop(NXY - 1, both_cores)
    send(piece, piece, last_send.at[0], last_recv.at[0], sibling)

    total_wait(gram_xy.at[pl.ds(0, NXY - 1)], one_recv.at[1])
    packed = gram_xy[0]
    for k in range(1, NXY):
        packed = packed + gram_xy[k]
    gram = jnp.concatenate([packed[:, q * RANK : (q + 1) * RANK] for q in range(PARTS)], 0)
    inverse = inverse_factor(gram)
    basis = exact(inverse, mine)
    solved[c, 0] = exact(inverse.T, basis)
    solved[c, 1] = jnp.concatenate([inverse.T, jnp.zeros((RANK, ROWS - RANK), F32)], 1)
    send(solved.at[c], solved.at[c], one_send.at[2], one_recv.at[2], sibling)

    def part_of(u):
        chunk, first, width = UNITS[u]
        return sums.at[c, pl.ds(chunk * RANKS, RANKS), pl.ds(first, width * NXY)]

    def hand(u):
        total_wait(t_xy.at[u, pl.ds(0, NXY - 1), :, : UNITS[u][2]], ag_recv.at[u])
        send(part_of(u), part_of(u), cp_send.at[u], cp_recv.at[u], sibling)

    loop(final, hand, True)

    total_wait(solved.at[other], one_recv.at[2])
    for m in range(2):
        both = jnp.concatenate([solved[m, 0].T, solved[m, 1].T[:RANK]], 0) * (1.0 / 16.0)
        hi, mid, lo = split3(both)
        left[m] = jnp.concatenate([hi, hi, mid, hi, mid, lo], 1)

    total_wait(gram_xy.at[pl.ds(0, NXY - 1)], one_send.at[1])
    total_wait(solved.at[c], one_send.at[2])
    for u, (chunk, first, width) in enumerate(UNITS):
        total_wait(t_z.at[u, pl.ds(0, NZ - 1), :, :width], tz_send.at[u])
        total_wait(t_xy.at[u, pl.ds(0, NXY - 1), :, :width], ag_send.at[u])
    total_wait(t_xy.at[0, :, :, : UNITS[final][2]], last_send.at[0])
    for u in range(final):
        total_wait(part_of(u), cp_recv.at[u])
        total_wait(part_of(u), cp_send.at[u])
    total_wait(t_xy.at[0, pl.ds(0, NXY - 1), :, : UNITS[final][2]], ag_recv.at[final])
    total_wait(t_xy.at[0, :, :, : UNITS[final][2]], last_recv.at[0])


def exchange(*args):
    vmem, sems = pltpu.VMEM, pltpu.SemaphoreType.DMA
    return pl.pallas_call(
        exchange_kernel,
        out_shape=(
            jax.ShapeDtypeStruct((2, RANK, COLS), F32),
            jax.ShapeDtypeStruct((2, ROWS + RANK, 6 * RANK), BF16),
            jax.ShapeDtypeStruct((2, ROWS, COLS), F32),
        ),
        in_specs=[pl.BlockSpec(memory_space=pltpu.HBM)] * 8,
        out_specs=[pl.BlockSpec(memory_space=pltpu.VMEM)] * 3,
        scratch_shapes=[
            vmem((2, ROWS, COLS), BF16),
            vmem((2, ROWS, COLS), BF16),
            vmem((2, COLS // BLOCK, ROWS), F32),
            vmem((2, RANK, COLS), F32),
            vmem((ROWS, COLS), F32),
            vmem((ROWS, COLS), BF16),
            vmem((ROWS, COLS), BF16),
            vmem((2, RANK, ROWS), F32),
            vmem((RANK, ROWS), F32),
            vmem((PARTS, NZ, RANKS, ROWS), F32),
            vmem((PARTS, RANKS, ROWS), F32),
            vmem((NXY, RANKS, RANK * PARTS), F32),
            vmem((2, 2, RANK, ROWS), F32),
            vmem((PARTS, RANKS, COLS), F32),
            vmem((len(UNITS), NXY, RANKS, PIECE), F32),
            vmem((len(UNITS), NZ, RANKS, PIECE), F32),
            sems((2, 2)),
            sems((2, LOADS, 2)),
            sems((3,)),
            sems((3,)),
            sems((CHUNKS,)),
            sems((CHUNKS,)),
        ]
        + [sems((len(UNITS),))] * 10
        + [sems((1,))] * 2,
        compiler_params=pltpu.CompilerParams(collective_id=0, has_side_effects=True, vmem_limit_bytes=28 << 20),
        cost_estimate=pl.CostEstimate(flops=1 << 30, bytes_accessed=8 << 20, transcendentals=0),
    )(*args)


def finish_kernel(
    sums, left, work,
    out0, out1, update0, update1, residue0, residue1,
    out_buf, update_buf, residue_buf, out_sems,
):
    outputs = ((out0, update0, residue0), (out1, update1, residue1))

    def part(k):
        cols = pl.ds(pl.multiple_of(k * SLICE, SLICE), SLICE)
        for m, (out, update, residue) in enumerate(outputs):
            hi, mid, lo = split3(sums[m, :, cols])
            both = mm(left[m], jnp.concatenate([hi, mid, hi, lo, mid, hi], 0))
            approx = both[:ROWS]
            update_buf[m, :, cols] = approx.astype(BF16)
            residue_buf[m, :, cols] = (work[m, :, cols] - approx).astype(BF16)
            out_buf[m, :, cols] = both[ROWS:]
            pltpu.make_async_copy(update_buf.at[m, :, cols], update.at[:, cols], out_sems.at[m, 0]).start()
            pltpu.make_async_copy(residue_buf.at[m, :, cols], residue.at[0, :, cols], out_sems.at[m, 1]).start()
            pltpu.make_async_copy(out_buf.at[m, :, cols], out.at[:, cols], out_sems.at[m, 2]).start()

    loop(SLICES, part)
    for m in range(2):
        total_wait(update_buf.at[m], out_sems.at[m, 0])
        total_wait(residue_buf.at[m], out_sems.at[m, 1])
        total_wait(out_buf.at[m], out_sems.at[m, 2])


def finish(sums, left, work):
    return pl.pallas_call(
        finish_kernel,
        out_shape=(
            jax.ShapeDtypeStruct((RANK, COLS), F32),
            jax.ShapeDtypeStruct((RANK, COLS), F32),
            jax.ShapeDtypeStruct((ROWS, COLS), BF16),
            jax.ShapeDtypeStruct((ROWS, COLS), BF16),
            jax.ShapeDtypeStruct((1, ROWS, COLS), BF16),
            jax.ShapeDtypeStruct((1, ROWS, COLS), BF16),
        ),
        in_specs=[pl.BlockSpec(memory_space=pltpu.VMEM)] * 3,
        out_specs=[pl.BlockSpec(memory_space=pltpu.HBM)] * 6,
        scratch_shapes=[
            pltpu.VMEM((2, RANK, COLS), F32),
            pltpu.VMEM((2, ROWS, COLS), BF16),
            pltpu.VMEM((2, ROWS, COLS), BF16),
            pltpu.SemaphoreType.DMA((2, 3)),
        ],
        compiler_params=pltpu.CompilerParams(vmem_limit_bytes=24 << 20),
    )(sums, left, work)


def shards(gate_grad, gate_scale, gate_error, gate_prior, up_grad, up_scale, up_error, up_prior):
    args = (
        gate_grad, gate_scale.transpose(0, 2, 1), gate_error, gate_prior.T,
        up_grad, up_scale.transpose(0, 2, 1), up_error, up_prior.T,
    )
    sums, left, work = exchange(*(pltpu.with_memory_space_constraint(a, pltpu.HBM) for a in args))
    columns0, columns1, update0, update1, residue0, residue1 = finish(sums, left, work)
    return (columns0.T, columns1.T, update0, update1, residue0, residue1)


def solution(mesh):
    in_specs = (
        P("dp", "tensor", None),
        P("dp", "tensor", None),
        P("dp", "tensor", None),
        P(),
        P("dp", "tensor", None),
        P("dp", "tensor", None),
        P("dp", "tensor", None),
        P(),
    )
    out_specs = (
        P(),
        P(),
        P("tensor", None),
        P("tensor", None),
        P("dp", "tensor", None),
        P("dp", "tensor", None),
    )
    return jax.shard_map(shards, mesh=mesh, in_specs=in_specs, out_specs=out_specs, check_vma=False)
```

```python
import jax
import jax.numpy as jnp
from jax import lax
from jax.experimental import pallas as pl
from jax.experimental.pallas import tpu as pltpu
from jax.sharding import PartitionSpec as P

MESH = pl.DeviceIdType.MESH
F32 = jnp.float32
BF16 = jnp.bfloat16

ROWS = 128
COLS = 4096
RANK = 32
BLOCK = 128
NZ = 8
NXY = 16
PARTS = 4
RANKS = RANK // PARTS
PIECE = COLS // NXY
HALF = PIECE // 2
UNITS = ((0, 0, PIECE), (1, 0, PIECE), (2, 0, PIECE), (3, 0, PIECE))
CHUNKS = 4
WIDTH = COLS // CHUNKS
LOADS = 2
LOAD = COLS // LOADS
SLICES = 8
SLICE = COLS // SLICES

FAR_Z = (4, 3, 5, 2, 6, 1, 7)
FAR_XY = (10, 6, 14, 9, 11, 5, 7, 13, 15, 2, 8, 1, 3, 4, 12)

NN = (((1,), (0,)), ((), ()))
NT = (((1,), (1,)), ((), ()))


def split2(a):
    hi = a.astype(BF16)
    lo = (a - hi.astype(F32)).astype(BF16)
    return hi, lo


def split3(a):
    hi = a.astype(BF16)
    rest = a - hi.astype(F32)
    mid = rest.astype(BF16)
    lo = (rest - mid.astype(F32)).astype(BF16)
    return hi, mid, lo


def mm(a, b, dims=NN):
    return lax.dot_general(a, b, dims, preferred_element_type=F32)


def exact(a, b, dims=NN):
    return lax.dot_general(a, b, dims, preferred_element_type=F32, precision=lax.Precision.HIGHEST)


def inverse_factor(gram):
    rows = lax.broadcasted_iota(jnp.int32, (RANK, 1), 0)
    eye = (lax.broadcasted_iota(jnp.int32, (RANK, RANK), 0) == lax.broadcasted_iota(jnp.int32, (RANK, RANK), 1)).astype(F32)
    left, right = gram, eye
    roots = jnp.zeros((RANK, 1), F32)
    for j in range(RANK):
        pivot = left[j : j + 1, j : j + 1]
        roots = jnp.where(rows == j, lax.rsqrt(pivot), roots)
        factor = jnp.where(rows > j, left[:, j : j + 1] / pivot, 0.0)
        left = left - factor * left[j : j + 1, :]
        right = right - factor * right[j : j + 1, :]
    return right * roots


def total_wait(ref, sem):
    pltpu.make_async_copy(ref, ref, sem).wait()


def send(ref, dst, send_sem, recv_sem, peer):
    pltpu.make_async_remote_copy(
        src_ref=ref, dst_ref=dst, send_sem=send_sem, recv_sem=recv_sem, device_id=peer, device_id_type=MESH
    ).start()


def loop(count, body, unroll=False):
    if count in (NXY - 1, NZ - 1, NZ):
        for i in range(count):
            body(i)
        return

    if unroll:
        for i in range(count):
            body(i)
        return
    lax.fori_loop(0, count, lambda i, carry: (body(i), carry)[1], 0)


def exchange_kernel(
    g0, s0, e0, p0, g1, s1, e1, p1,
    sums, left, work,
    g_buf, e_buf, s_buf, p_buf, w_pair, u_hi, u_lo,
    f_part, f_pair, f_z, f_all, gram_xy, solved,
    t_own, t_xy, t_z,
    small_sems, in_sems, one_send, one_recv, w_send, w_recv, fz_send, fz_recv,
    rs_send, rs_recv, tz_send, tz_recv, ag_send, ag_recv, cp_send, cp_recv, last_send, last_recv,
):
    dp = lax.axis_index("dp")
    me = lax.axis_index("tensor")
    z, c = dp // 2, dp % 2
    x, y = me // 4, me % 4
    other = 1 - c
    sibling = {"dp": z * 2 + other, "tensor": me}

    z_bases = [lax.rem(z + k, NZ) * 2 for k in FAR_Z + (0,)]
    xy_all = [lax.rem(x + k // 4, 4) * 4 + lax.rem(y + k % 4, 4) for k in FAR_XY]

    def z_peer(i):
        return {"dp": z_bases[i] + c, "tensor": me}

    def z_cross(i):
        return {"dp": z_bases[i] + other, "tensor": me}

    def xy_index(i):
        return xy_all[i]

    def xy_peer(i):
        return {"dp": dp, "tensor": xy_index(i)}

    def xy_cross(i):
        return {"dp": z * 2 + other, "tensor": xy_index(i)}

    refs = ((g0, s0, e0, p0), (g1, s1, e1, p1))
    for m, (g, sc, e, p) in enumerate(refs):
        pltpu.make_async_copy(sc.at[0], s_buf.at[m], small_sems.at[m, 0]).start()
        pltpu.make_async_copy(p, p_buf.at[m], small_sems.at[m, 1]).start()

    def fetch(k):
        cols = pl.ds(k * LOAD, LOAD)
        for m, (g, sc, e, p) in enumerate(refs):
            pltpu.make_async_copy(g.at[0, :, cols], g_buf.at[m, :, cols], in_sems.at[m, k, 0]).start()
            pltpu.make_async_copy(e.at[0, :, cols], e_buf.at[m, :, cols], in_sems.at[m, k, 1]).start()

    fetch(0)
    barrier = pltpu.get_barrier_semaphore()

    def greet(peer):
        pl.semaphore_signal(barrier, inc=1, device_id=peer, device_id_type=MESH)

    loop(NZ - 1, lambda i: greet(z_peer(i)))
    greet(sibling)
    loop(NXY - 1, lambda i: greet(xy_peer(i)))
    for k in range(1, LOADS):
        fetch(k)

    for m in range(2):
        total_wait(s_buf.at[m], small_sems.at[m, 0])
        total_wait(p_buf.at[m], small_sems.at[m, 1])

    def partial(k, totals):
        cols = pl.ds(pl.multiple_of(k * LOAD, LOAD), LOAD)
        count = LOAD // BLOCK
        for m in range(2):
            total_wait(g_buf.at[m, :, cols], in_sems.at[m, k, 0])
            total_wait(e_buf.at[m, :, cols], in_sems.at[m, k, 1])
        result = []
        zero = jnp.zeros((2 * RANK, BLOCK), BF16)
        lower = lax.broadcasted_iota(jnp.int32, (ROWS, 4 * RANK), 1) < 2 * RANK
        for m in range(2):
            total = totals[m]
            scale = s_buf[m, pl.ds(pl.multiple_of(k * count, count), count), :].T
            for b in range(0, count, 2):
                at = pl.ds(pl.multiple_of(k * LOAD + b * BLOCK, 2 * BLOCK), 2 * BLOCK)
                hi, lo = split2(p_buf[m, :, at])
                prior = jnp.concatenate([hi, lo], 0)
                even = jnp.concatenate([prior[:, :BLOCK], zero], 1)
                odd = jnp.concatenate([zero, prior[:, BLOCK:]], 1)
                both = jnp.concatenate([g_buf[m, :, at], e_buf[m, :, at]], 0)
                out = mm(both, jnp.concatenate([even, odd], 0), NT)
                pair = jnp.where(lower, scale[:, b : b + 1], scale[:, b + 1 : b + 2])
                total = total + (out[:ROWS] * pair + out[ROWS:])
            result.append(total)
        return tuple(result)

    start = jnp.zeros((ROWS, 128), F32)
    totals = lax.fori_loop(0, LOADS, partial, (start, start))
    for m in range(2):
        total = totals[m]
        folded = total[:, : 2 * RANK] + total[:, 2 * RANK :]
        factor = folded[:, :RANK] + folded[:, RANK:]
        f_part[m] = factor.T

    pl.semaphore_wait(barrier, NZ + (NXY - 1))

    send(f_part.at[other], f_pair, one_send.at[0], one_recv.at[0], sibling)

    def spread(q):
        f_z[q, z] = f_part[c, q * RANKS : (q + 1) * RANKS] + f_pair[q * RANKS : (q + 1) * RANKS]
        loop(NZ - 1, lambda i: send(f_z.at[q, z], f_z.at[q, z], fz_send.at[q], fz_recv.at[q], z_peer(i)))

    def values(m, k):
        count = WIDTH // BLOCK
        scale = s_buf[m, pl.ds(pl.multiple_of(k * count, count), count), :].T
        for b in range(count):
            at = pl.ds(pl.multiple_of(k * WIDTH + b * BLOCK, BLOCK), BLOCK)
            work[m, :, at] = g_buf[m, :, at].astype(F32) * scale[:, b : b + 1] + e_buf[m, :, at].astype(F32)

    def chunk_of(k):
        return pl.ds(pl.multiple_of(k * WIDTH, WIDTH), WIDTH)

    def give(k):
        values(other, k)
        cols = chunk_of(k)
        send(work.at[other, :, cols], w_pair.at[:, cols], w_send.at[k], w_recv.at[k], sibling)

    give(0)
    give(1)
    total_wait(f_pair, one_recv.at[0])
    for q in range(PARTS):
        spread(q)
    lax.fori_loop(2, CHUNKS, lambda k, carry: (give(k), carry)[1], 0)

    loop(CHUNKS, lambda k: values(c, k))

    def take(k):
        cols = chunk_of(k)
        total_wait(w_pair.at[:, cols], w_recv.at[k])
        hi, lo = split2(work[c, :, cols] + w_pair[:, cols])
        u_hi[:, cols] = hi
        u_lo[:, cols] = lo

    loop(CHUNKS, take)
    total_wait(f_pair, one_send.at[0])
    loop(CHUNKS, lambda k: total_wait(w_pair.at[:, chunk_of(k)], w_send.at[k]))

    def flow(q):
        total_wait(f_z.at[q, pl.ds(0, NZ - 1)], fz_recv.at[q])
        total = f_z[q, 0]
        for k in range(1, NZ):
            total = total + f_z[q, k]
        f_all[q] = total
        hi, lo = split2(total)
        lhs = jnp.concatenate([jnp.concatenate([hi, hi], 1), jnp.concatenate([lo, jnp.zeros_like(lo)], 1)], 0)
        both = mm(lhs, jnp.concatenate([u_hi[...], u_lo[...]], 0))
        t_own[q] = both[:RANKS] + both[RANKS:]

        for u, (chunk, first, width) in enumerate(UNITS):
            if chunk == q:
                for j in range(NXY - 1):
                    cols = pl.ds(pl.multiple_of(first + xy_index(j) * width, width), width)
                    send(t_own.at[q, :, cols], t_xy.at[u, me, :, :width], rs_send.at[u], rs_recv.at[u], xy_peer(j))
                t_xy[u, me, :, :width] = t_own[q, :, pl.ds(pl.multiple_of(first + me * width, width), width)]

    loop(PARTS, flow, True)

    mine = jnp.concatenate([f_all[q] for q in range(PARTS)], 0)
    gram = exact(mine, mine, NT)
    gram_xy[me] = jnp.concatenate([gram[q * RANKS : (q + 1) * RANKS] for q in range(PARTS)], 1)
    loop(NXY - 1, lambda j: send(gram_xy.at[me], gram_xy.at[me], one_send.at[1], one_recv.at[1], xy_peer(j)))

    def middle(q):
        width = UNITS[q][2]
        total_wait(t_xy.at[q, pl.ds(0, NXY - 1), :, :width], rs_recv.at[q])
        total = t_xy[q, 0, :, :width]
        for k in range(1, NXY):
            total = total + t_xy[q, k, :, :width]
        t_z[q, z, :, :width] = total
        piece = t_z.at[q, z, :, :width]
        loop(NZ - 1, lambda i: send(piece, piece, tz_send.at[q], tz_recv.at[q], z_peer(i)))

    loop(len(UNITS), middle, True)
    loop(PARTS, lambda q: total_wait(f_z.at[q, pl.ds(0, NZ - 1)], fz_send.at[q]))
    for u, (chunk, first, width) in enumerate(UNITS):
        total_wait(t_xy.at[u, pl.ds(0, NXY - 1), :, :width], rs_send.at[u])

    def collect(u):
        chunk, first, width = UNITS[u]
        total_wait(t_z.at[u, pl.ds(0, NZ - 1), :, :width], tz_recv.at[u])
        total = t_z[u, 0, :, :width]
        for k in range(1, NZ):
            total = total + t_z[u, k, :, :width]
        rows = pl.ds(chunk * RANKS, RANKS)
        cols = pl.ds(pl.multiple_of(first + me * width, width), width)
        sums[c, rows, cols] = total
        return sums.at[c, rows, cols]

    def gather(u):
        piece = collect(u)
        loop(NXY - 1, lambda j: send(piece, piece, ag_send.at[u], ag_recv.at[u], xy_peer(j)))

    final = len(UNITS) - 1
    loop(final, gather, True)
    piece = collect(final)

    def both_cores(j):
        send(piece, piece, ag_send.at[final], ag_recv.at[final], xy_peer(j))
        send(piece, piece, last_send.at[0], last_recv.at[0], xy_cross(j))

    loop(NXY - 1, both_cores)
    send(piece, piece, last_send.at[0], last_recv.at[0], sibling)

    total_wait(gram_xy.at[pl.ds(0, NXY - 1)], one_recv.at[1])
    packed = gram_xy[0]
    for k in range(1, NXY):
        packed = packed + gram_xy[k]
    gram = jnp.concatenate([packed[:, q * RANK : (q + 1) * RANK] for q in range(PARTS)], 0)
    inverse = inverse_factor(gram)
    basis = exact(inverse, mine)
    solved[c, 0] = exact(inverse.T, basis)
    solved[c, 1] = jnp.concatenate([inverse.T, jnp.zeros((RANK, ROWS - RANK), F32)], 1)
    send(solved.at[c], solved.at[c], one_send.at[2], one_recv.at[2], sibling)

    def part_of(u):
        chunk, first, width = UNITS[u]
        return sums.at[c, pl.ds(chunk * RANKS, RANKS), pl.ds(first, width * NXY)]

    def hand(u):
        total_wait(t_xy.at[u, pl.ds(0, NXY - 1), :, : UNITS[u][2]], ag_recv.at[u])
        send(part_of(u), part_of(u), cp_send.at[u], cp_recv.at[u], sibling)

    loop(final, hand, True)

    total_wait(solved.at[other], one_recv.at[2])
    for m in range(2):
        both = jnp.concatenate([solved[m, 0].T, solved[m, 1].T[:RANK]], 0) * (1.0 / 16.0)
        hi, mid, lo = split3(both)
        left[m] = jnp.concatenate([hi, hi, mid, hi, mid, lo], 1)

    total_wait(gram_xy.at[pl.ds(0, NXY - 1)], one_send.at[1])
    total_wait(solved.at[c], one_send.at[2])
    for u, (chunk, first, width) in enumerate(UNITS):
        total_wait(t_z.at[u, pl.ds(0, NZ - 1), :, :width], tz_send.at[u])
        total_wait(t_xy.at[u, pl.ds(0, NXY - 1), :, :width], ag_send.at[u])
    total_wait(t_xy.at[0, :, :, : UNITS[final][2]], last_send.at[0])
    for u in range(final):
        total_wait(part_of(u), cp_recv.at[u])
        total_wait(part_of(u), cp_send.at[u])
    total_wait(t_xy.at[0, pl.ds(0, NXY - 1), :, : UNITS[final][2]], ag_recv.at[final])
    total_wait(t_xy.at[0, :, :, : UNITS[final][2]], last_recv.at[0])


def exchange(*args):
    vmem, sems = pltpu.VMEM, pltpu.SemaphoreType.DMA
    return pl.pallas_call(
        exchange_kernel,
        out_shape=(
            jax.ShapeDtypeStruct((2, RANK, COLS), F32),
            jax.ShapeDtypeStruct((2, ROWS + RANK, 6 * RANK), BF16),
            jax.ShapeDtypeStruct((2, ROWS, COLS), F32),
        ),
        in_specs=[pl.BlockSpec(memory_space=pltpu.HBM)] * 8,
        out_specs=[pl.BlockSpec(memory_space=pltpu.VMEM)] * 3,
        scratch_shapes=[
            vmem((2, ROWS, COLS), BF16),
            vmem((2, ROWS, COLS), BF16),
            vmem((2, COLS // BLOCK, ROWS), F32),
            vmem((2, RANK, COLS), F32),
            vmem((ROWS, COLS), F32),
            vmem((ROWS, COLS), BF16),
            vmem((ROWS, COLS), BF16),
            vmem((2, RANK, ROWS), F32),
            vmem((RANK, ROWS), F32),
            vmem((PARTS, NZ, RANKS, ROWS), F32),
            vmem((PARTS, RANKS, ROWS), F32),
            vmem((NXY, RANKS, RANK * PARTS), F32),
            vmem((2, 2, RANK, ROWS), F32),
            vmem((PARTS, RANKS, COLS), F32),
            vmem((len(UNITS), NXY, RANKS, PIECE), F32),
            vmem((len(UNITS), NZ, RANKS, PIECE), F32),
            sems((2, 2)),
            sems((2, LOADS, 2)),
            sems((3,)),
            sems((3,)),
            sems((CHUNKS,)),
            sems((CHUNKS,)),
        ]
        + [sems((len(UNITS),))] * 10
        + [sems((1,))] * 2,
        compiler_params=pltpu.CompilerParams(collective_id=0, has_side_effects=True, vmem_limit_bytes=28 << 20),
        cost_estimate=pl.CostEstimate(flops=1 << 30, bytes_accessed=8 << 20, transcendentals=0),
    )(*args)


def finish_kernel(
    sums, left, work,
    out0, out1, update0, update1, residue0, residue1,
    out_buf, update_buf, residue_buf, out_sems,
):
    outputs = ((out0, update0, residue0), (out1, update1, residue1))

    def part(k):
        cols = pl.ds(pl.multiple_of(k * SLICE, SLICE), SLICE)
        for m, (out, update, residue) in enumerate(outputs):
            hi, mid, lo = split3(sums[m, :, cols])
            both = mm(left[m], jnp.concatenate([hi, mid, hi, lo, mid, hi], 0))
            approx = both[:ROWS]
            update_buf[m, :, cols] = approx.astype(BF16)
            residue_buf[m, :, cols] = (work[m, :, cols] - approx).astype(BF16)
            out_buf[m, :, cols] = both[ROWS:]
            pltpu.make_async_copy(update_buf.at[m, :, cols], update.at[:, cols], out_sems.at[m, 0]).start()
            pltpu.make_async_copy(residue_buf.at[m, :, cols], residue.at[0, :, cols], out_sems.at[m, 1]).start()
            pltpu.make_async_copy(out_buf.at[m, :, cols], out.at[:, cols], out_sems.at[m, 2]).start()

    loop(SLICES, part)
    for m in range(2):
        total_wait(update_buf.at[m], out_sems.at[m, 0])
        total_wait(residue_buf.at[m], out_sems.at[m, 1])
        total_wait(out_buf.at[m], out_sems.at[m, 2])


def finish(sums, left, work):
    return pl.pallas_call(
        finish_kernel,
        out_shape=(
            jax.ShapeDtypeStruct((RANK, COLS), F32),
            jax.ShapeDtypeStruct((RANK, COLS), F32),
            jax.ShapeDtypeStruct((ROWS, COLS), BF16),
            jax.ShapeDtypeStruct((ROWS, COLS), BF16),
            jax.ShapeDtypeStruct((1, ROWS, COLS), BF16),
            jax.ShapeDtypeStruct((1, ROWS, COLS), BF16),
        ),
        in_specs=[pl.BlockSpec(memory_space=pltpu.VMEM)] * 3,
        out_specs=[pl.BlockSpec(memory_space=pltpu.HBM)] * 6,
        scratch_shapes=[
            pltpu.VMEM((2, RANK, COLS), F32),
            pltpu.VMEM((2, ROWS, COLS), BF16),
            pltpu.VMEM((2, ROWS, COLS), BF16),
            pltpu.SemaphoreType.DMA((2, 3)),
        ],
        compiler_params=pltpu.CompilerParams(vmem_limit_bytes=24 << 20),
    )(sums, left, work)


def shards(gate_grad, gate_scale, gate_error, gate_prior, up_grad, up_scale, up_error, up_prior):
    args = (
        gate_grad, gate_scale.transpose(0, 2, 1), gate_error, gate_prior.T,
        up_grad, up_scale.transpose(0, 2, 1), up_error, up_prior.T,
    )
    sums, left, work = exchange(*(pltpu.with_memory_space_constraint(a, pltpu.HBM) for a in args))
    columns0, columns1, update0, update1, residue0, residue1 = finish(sums, left, work)
    return (columns0.T, columns1.T, update0, update1, residue0, residue1)


def solution(mesh):
    in_specs = (
        P("dp", "tensor", None),
        P("dp", "tensor", None),
        P("dp", "tensor", None),
        P(),
        P("dp", "tensor", None),
        P("dp", "tensor", None),
        P("dp", "tensor", None),
        P(),
    )
    out_specs = (
        P(),
        P(),
        P("tensor", None),
        P("tensor", None),
        P("dp", "tensor", None),
        P("dp", "tensor", None),
    )
    return jax.shard_map(shards, mesh=mesh, in_specs=in_specs, out_specs=out_specs, check_vma=False)
```
